128 devices in a mesh: node: 32 (over z, y, core), rep: 4 (over x).
Axes of the slice: x: 4, y: 4, z: 4, core: 2. Of those that a mesh axis runs over, the one named last changes fastest.
Arguments:
- embeddings: bfloat16 [262144, 512], P(('node', 'rep')), may hold values from -6 to 6
- w_first: bfloat16 [512, 512], replicated, may hold values from -0.25 to 0.25
- w_second: bfloat16 [512, 512], replicated, may hold values from -0.25 to 0.25
- w_score: bfloat16 [512], replicated, may hold values from -0.5 to 0.5
- src_row: int32 [65536], P(('node', 'rep')), may hold values from 0 to 2047
- dst_owner: int32 [65536, 1], P(('node', 'rep')), may hold values from 0 to 127; in each aligned block of 512 rows (0 to 511, 512 to 1023, ...) at most 8 rows name the same one
- dst_row: int32 [65536], P(('node', 'rep')), may hold values from 0 to 2047
- edge_count: int32 [128], replicated, may hold values from 1 to 512, as said below
- neg_ids: int32 [8], replicated, may hold values from 0 to 262143
Outputs:
- grad_embeddings: float32 [262144, 512], P(('node', 'rep'))
- grad_first: float32 [512, 512], replicated
- grad_second: float32 [512, 512], replicated
- grad_score: float32 [512], replicated
- loss: float32 [], replicated
The draws below stay inside these ranges and needn't reach their ends.
Inputs may be any that keep to these rules, and one draw needn't show every extreme that they name: `dst_owner`: among the 512 slots of one device no owner is named more than 8 times, a bound that some block reaches. `edge_count`: some device has all 512 slots live.
All inputs are finite; a program needn't handle non-finite values.
Results may differ from the reference program's by a relative error of at most 0.0035.
Values may be sent and summed in bfloat16 or wider, within the bound.
No kernel may reach another device: no remote copies, remote signals or barrier semaphores. Data moves between devices by JAX's collectives and lax.ppermute only.
A program may use at most 128 MiB of HBM per device.

```python
import math
import jax
import jax.numpy as jnp
import numpy as np
from jax import lax

D = 512
ROWS_DEV = 2048
E_DEV = 512
NEG = 8
CAP = 8
NODES = 262144
EDGES = 65536
DEVICES = 128


def draw_edge_count(key, part):
    key = jax.random.fold_in(key, 11)
    shifts = jax.random.randint(jax.random.fold_in(key, 1), (DEVICES,), 0, 4)
    base = jnp.right_shift(jnp.full((DEVICES,), E_DEV, jnp.int32), shifts.astype(jnp.int32))
    jitter = jax.random.randint(jax.random.fold_in(key, 2), (DEVICES,), 0, E_DEV // 16 + 1)
    counts = jnp.maximum(base - jitter, 1).astype(jnp.int32)
    chosen = jax.random.randint(jax.random.fold_in(key, 3), (), 0, DEVICES)
    return counts.at[chosen].set(E_DEV).astype(jnp.int32)


def set_ends(result, own_key, smallest, high):
    shape = result.shape
    spot = [jax.random.randint(jax.random.fold_in(own_key, axis), (), 0, shape[axis]) for axis in range(len(shape))]
    result = result.at[tuple(spot)].set(smallest)
    longest = shape.index(max(shape))
    spot[longest] = (spot[longest] + 1) % shape[longest]
    return result.at[tuple(spot)].set(high)


def block_levels(key, dims, cuts, least, top_value):
    def one(dim, parts):
        heights = jax.random.uniform(jax.random.fold_in(jax.random.fold_in(key, 6), dim), (parts,), jnp.float32, least / len(cuts), top_value / len(cuts))
        return jnp.repeat(jnp.exp(heights), dims[dim] // parts).reshape((-1,) + (1,) * (len(dims) - dim - 1))

    gain = one(*cuts[0])
    for cut in cuts[1:]:
        gain = gain * one(*cut)
    return gain


def routed_block(rng, own, number, rows, amount, top, most, skew):
    order = jax.random.permutation(rng, amount)
    crowded, ordinary = portions_of(amount, rows * top, most, skew, True), portions_of(amount, rows * top, most, skew, False)
    places = jnp.arange(amount)

    def named(tallies, offset_by):
        used = int((tallies > 0).sum())
        fixed = max(1, used // 4)
        moved = fixed + (places - fixed + offset_by * (used - fixed)) % max(1, amount - fixed)
        return jnp.zeros((amount,), jnp.int32).at[order[jnp.where(places < fixed, places, moved)]].set(jnp.asarray(tallies, jnp.int32))

    tallies = jnp.where(number % 4 == 0, named(crowded, number // 4), named(ordinary, number - number // 4 - 1))
    mixed = jax.random.permutation(jax.random.fold_in(own, 3), amount)
    source_of, sink = mixed[0:amount // 2 * 2:2], mixed[1:amount // 2 * 2:2]
    slack = jnp.minimum(tallies[source_of] - 1, most - tallies[sink]) // 2
    slack = jnp.where((source_of == order[0]) | (sink == order[0]) | (tallies[sink] == 0), 0, jnp.maximum(slack, 0))
    moved = jax.random.randint(jax.random.fold_in(own, 4), (amount // 2,), 0, 1 << 20) % (slack + 1)
    tallies = tallies.at[source_of].add(-moved).at[sink].add(moved)
    labels = jnp.searchsorted(jnp.cumsum(tallies), jnp.arange(rows * top), side="right").astype(jnp.int32)
    listing = labels.reshape(top, rows).T
    listing = listing[jax.random.permutation(jax.random.fold_in(own, 1), rows)]
    offset_by = jax.random.randint(jax.random.fold_in(own, 2), (rows, 1), 0, top)
    return jnp.take_along_axis(listing, (jnp.arange(top)[None, :] + offset_by) % top, axis=1)


def portions_of(number_of, total, bound, skew, full):
    loads = [(1 << 20) // math.isqrt(rank ** skew) + 1 for rank in range(1, number_of + 1)]
    largest = bound if full else min(bound, max(-(-total // number_of), total * loads[0] // sum(loads)))
    least = 1 if total - largest >= number_of - 1 else 0
    given, spare = [largest] + [least] * (number_of - 1), total - largest - least * (number_of - 1)
    while spare > 0:
        movable = [i for i in range(1, number_of) if given[i] < largest] or [i for i in range(1, number_of) if given[i] < bound]
        mass, budget = sum([loads[i] for i in movable]), spare
        for i in movable:
            extra = min(bound - given[i], max(1, budget * loads[i] // mass), spare)
            given[i] = given[i] + extra
            spare = spare - extra
    return np.array(given)


def bell_draw(rng, extent, scale, most, split=(), held_as=jnp.bfloat16):
    drawn = scale * jax.random.normal(rng, extent, jnp.float32)
    if split:
        drawn = drawn * block_levels(rng, extent, split, -0.22, 0.18)
    return jnp.clip(drawn, -most, most).astype(held_as)


def setup_inputs(seed: int = 0) -> dict:
    key_of = jax.random.split(jax.random.key(seed), 10)
    embeddings = bell_draw(key_of[0], (NODES, D), 1.0, 6.0, ((0, 128),))
    w_first = bell_draw(key_of[1], (D, D), D ** -0.5, 0.25)
    w_second = bell_draw(key_of[2], (D, D), D ** -0.5, 0.25)
    w_score = bell_draw(key_of[3], (D,), (D // 4) ** -0.5, 0.5)
    src_row = set_ends(jax.random.randint(key_of[4], (EDGES,), 0, ROWS_DEV), jax.random.fold_in(key_of[4], 1), 0, ROWS_DEV - 1).astype(jnp.int32)
    dst_owner_keys = jax.random.split(jax.random.fold_in(key_of[5], 1), EDGES // E_DEV)
    dst_owner_turns = jax.random.permutation(jax.random.fold_in(key_of[5], 3), EDGES // E_DEV)
    dst_owner = jax.vmap(lambda own, number: routed_block(jax.random.fold_in(key_of[5], 2), own, number, E_DEV, DEVICES, 1, CAP, 2))(dst_owner_keys, dst_owner_turns).reshape((EDGES, 1))
    dst_row = set_ends(jax.random.randint(key_of[6], (EDGES,), 0, ROWS_DEV), jax.random.fold_in(key_of[6], 1), 0, ROWS_DEV - 1).astype(jnp.int32)
    edge_count = draw_edge_count(jax.random.fold_in(key_of[9], 71), 0)
    neg_ids = set_ends(jax.random.randint(key_of[8], (NEG,), 0, NODES), jax.random.fold_in(key_of[8], 1), 0, NODES - 1).astype(jnp.int32)
    return {"embeddings": embeddings, "w_first": w_first, "w_second": w_second, "w_score": w_score, "src_row": src_row, "dst_owner": dst_owner, "dst_row": dst_row, "edge_count": edge_count, "neg_ids": neg_ids}


def silu_slope(value):
    sig = jax.nn.sigmoid(value)
    return sig * (1.0 + value * (1.0 - sig))


def decode(src_emb, dst_emb, negatives, w_first, w_second, w_score, live, total):
    edges = src_emb.shape[0]
    width = src_emb.shape[1]
    count_neg = negatives.shape[0]
    src_f = src_emb.astype(jnp.float32)
    dst_f = dst_emb.astype(jnp.float32)
    neg_f = negatives.astype(jnp.float32)
    x_pos = (src_f * dst_f).astype(jnp.bfloat16)
    x_neg = (src_f[:, None, :] * neg_f[None, :, :]).reshape(edges * count_neg, width).astype(jnp.bfloat16)
    stacked = jnp.concatenate([x_pos, x_neg], axis=0)
    z_one = jnp.dot(stacked, w_first, preferred_element_type=jnp.float32)
    a_one = jax.nn.silu(z_one).astype(jnp.bfloat16)
    z_two = jnp.dot(a_one, w_second, preferred_element_type=jnp.float32)
    a_two = jax.nn.silu(z_two).astype(jnp.bfloat16)
    score = jnp.dot(a_two, w_score, preferred_element_type=jnp.float32)
    pos_score = score[:edges]
    neg_score = score[edges:].reshape(edges, count_neg)
    loss = (jnp.sum(live * jax.nn.softplus(-pos_score)) + jnp.sum(live[:, None] * jax.nn.softplus(neg_score)) / count_neg) / total
    ds_pos = -jax.nn.sigmoid(-pos_score) * live / total
    ds_neg = jax.nn.sigmoid(neg_score) * live[:, None] / (count_neg * total)
    slope = jnp.concatenate([ds_pos, ds_neg.reshape(-1)], axis=0)
    grad_score = jnp.dot(slope, a_two, preferred_element_type=jnp.float32)
    dz_two = (slope[:, None] * w_score.astype(jnp.float32)[None, :] * silu_slope(z_two)).astype(jnp.bfloat16)
    grad_second = jnp.dot(a_one.T, dz_two, preferred_element_type=jnp.float32)
    dz_one = (jnp.dot(dz_two, w_second.T, preferred_element_type=jnp.float32) * silu_slope(z_one)).astype(jnp.bfloat16)
    grad_first = jnp.dot(stacked.T, dz_one, preferred_element_type=jnp.float32)
    d_input = jnp.dot(dz_one, w_first.T, preferred_element_type=jnp.float32)
    dx_pos = d_input[:edges]
    dx_neg = d_input[edges:].reshape(edges, count_neg, width)
    grad_src = dx_pos * dst_f + jnp.einsum("ekd,kd->ed", dx_neg, neg_f)
    grad_dst = dx_pos * src_f
    grad_neg = jnp.einsum("ekd,ed->kd", dx_neg, src_f)
    return grad_src, grad_dst, grad_neg, grad_first, grad_second, grad_score, loss


def reference(embeddings, w_first, w_second, w_score, src_row, dst_owner, dst_row, edge_count, neg_ids):
    total = jnp.sum(edge_count).astype(jnp.float32)
    negatives = embeddings[neg_ids]
    slots = jnp.arange(E_DEV, dtype=jnp.int32)

    def one_device(carry, device):
        grads, g_first, g_second, g_score, g_neg, loss = carry
        begin = (device * E_DEV).astype(jnp.int32)
        rows_src = lax.dynamic_slice_in_dim(src_row, begin, E_DEV, 0)
        owners = lax.dynamic_slice_in_dim(dst_owner[:, 0], begin, E_DEV, 0)
        rows_dst = lax.dynamic_slice_in_dim(dst_row, begin, E_DEV, 0)
        src_ids = (device * ROWS_DEV + rows_src).astype(jnp.int32)
        dst_ids = (owners * ROWS_DEV + rows_dst).astype(jnp.int32)
        live = (slots < edge_count[device]).astype(jnp.float32)
        outs = decode(embeddings[src_ids], embeddings[dst_ids], negatives, w_first, w_second, w_score, live, total)
        grads = grads.at[src_ids].add(outs[0]).at[dst_ids].add(outs[1])
        return (grads, g_first + outs[3], g_second + outs[4], g_score + outs[5], g_neg + outs[2], loss + outs[6]), None

    start = (jnp.zeros((NODES, D), jnp.float32), jnp.zeros((D, D), jnp.float32), jnp.zeros((D, D), jnp.float32),
             jnp.zeros((D,), jnp.float32), jnp.zeros((NEG, D), jnp.float32), jnp.zeros((), jnp.float32))
    final, unused = lax.scan(one_device, start, jnp.arange(DEVICES, dtype=jnp.int32))
    grads, g_first, g_second, g_score, g_neg, loss = final
    grads = grads.at[neg_ids].add(g_neg)
    return grads, g_first, g_second, g_score, loss
```

```python
import jax
import jax.numpy as jnp
from jax import lax
from jax.experimental import pallas as pl
from jax.experimental.pallas import tpu as pltpu
from jax.sharding import Mesh, PartitionSpec as P

F32 = jnp.float32
BF16 = jnp.bfloat16
AXES = ("z", "y", "c", "x")
CHIPS = ("z", "y", "x")
VMEM = pl.BlockSpec(memory_space=pltpu.VMEM)
SMEM = pl.BlockSpec(memory_space=pltpu.SMEM)
HBM = pl.BlockSpec(memory_space=pltpu.HBM)
MIB = 1 << 20


def in_hbm(*arrays):
    return tuple(pltpu.with_memory_space_constraint(a, pltpu.HBM) for a in arrays)


DEVICES = 128
GROUP = 64
ROWS = 2048
EDGES = 512
WIDTH = 512
NEG = 8
CAP = 8
SLOTS = DEVICES * CAP
LANES = 128
WIDE = WIDTH + LANES
TALL = WIDTH + 16


def mm(a, b):
    return jnp.dot(a, b, preferred_element_type=F32)


def mm_nt(a, b):
    return lax.dot_general(a, b, (((1,), (1,)), ((), ())), preferred_element_type=F32)


def mm_tn(a, b):
    return lax.dot_general(a, b, (((0,), (0,)), ((), ())), preferred_element_type=F32)


def wide(value):
    return jnp.concatenate([value] * (WIDTH // LANES), axis=1)


def iota(shape, dim):
    return lax.broadcasted_iota(jnp.int32, shape, dim)


def one(mask):
    return jnp.where(mask, 1.0, 0.0).astype(BF16)


def column(row):
    return jnp.transpose(jnp.broadcast_to(row.astype(F32), (LANES, row.shape[1]))).astype(jnp.int32)


def onehot_rows(col, count):
    lane = iota(col.shape, 1)
    return jnp.concatenate([one(col == lane + LANES * j) for j in range(count // LANES)], axis=1)


def split(value):
    high = value.astype(BF16)
    return high, (value - high.astype(F32)).astype(BF16)


def softplus(value):
    return jnp.maximum(value, 0.0) + jnp.log1p(jnp.exp(-jnp.abs(value)))


def gate(half):
    t = jnp.tanh(half)
    m = half * t
    return half + m, (1.0 + t) * (1.0 + (half - m))


def counts(ec_ref):
    me = lax.axis_index(AXES)
    ec = ec_ref[...]
    mine = jnp.sum(jnp.where(iota(ec.shape, 1) == me, ec, 0).astype(F32), axis=1, keepdims=True)
    return mine, jnp.sum(ec.astype(F32), axis=1, keepdims=True)


def prepare_kernel(emb_hbm, src_hbm, owner_hbm, dst_hbm, ec_hbm, neg_hbm, push_ref, semb_hbm, pos_ref,
                   emb_ref, src_ref, owner_ref, dst_ref, ec_ref, neg_ref, semb_ref, sems):
    pairs = [(neg_hbm, neg_ref), (ec_hbm, ec_ref), (owner_hbm, owner_ref), (src_hbm, src_ref),
             (dst_hbm, dst_ref), (emb_hbm, emb_ref)]
    copies = [pltpu.make_async_copy(a, b, sems.at[i]) for i, (a, b) in enumerate(pairs)]
    for copy in copies:
        copy.start()
    for copy in copies[:-1]:
        copy.wait()
    me = lax.axis_index(AXES)
    mine, _ = counts(ec_ref)
    live = iota((1, EDGES), 1).astype(F32) < mine
    owner = jnp.where(live, owner_ref[...], -1)
    named = one(iota((DEVICES, EDGES), 0) == owner)
    before = one(iota((EDGES, EDGES), 0) < iota((EDGES, EDGES), 1))
    rank = jnp.sum(mm(named, before) * named.astype(F32), axis=0, keepdims=True)
    pos = jnp.where(live, owner * CAP + rank.astype(jnp.int32), -1)
    pos_ref[...] = pos
    row = column(dst_ref[...])
    lane = iota((EDGES, LANES), 1)
    meta = jnp.where(lane == 0, row // 64, jnp.where(lane == 1, row % 64, jnp.where(lane == 2, 1, 0)))
    meta = meta.astype(F32).astype(BF16)
    sub = iota((NEG, LANES), 0)
    local = jnp.zeros((NEG, LANES), jnp.int32)
    for k in range(NEG):
        local = jnp.where(sub == k, neg_ref[k] - me * ROWS, local)
    offered = onehot_rows(local, ROWS)
    chosen = onehot_rows(column(src_ref[...]), ROWS)
    copies[-1].wait()
    emb = emb_ref[...]
    semb = mm(chosen, emb).astype(BF16)
    semb_ref[...] = semb
    out = pltpu.make_async_copy(semb_ref, semb_hbm, sems.at[6])
    out.start()
    offers = mm(offered, emb)
    high = iota((NEG, LANES), 1) >= LANES // 2
    pieces = []
    for q in range(4):
        tile = offers[:, LANES * q:LANES * (q + 1)]
        pieces += [jnp.where(high, pltpu.roll(tile, LANES // 2, 1), 0.0), jnp.where(high, tile, 0.0)]
    pieces = jnp.concatenate(pieces, axis=0)
    count = SLOTS // 4
    for q in range(4):
        rows = pl.ds(q * count, count)
        place = one(iota((count, EDGES), 0) + q * count == pos)
        push_ref[rows, 0:WIDTH] = mm(place, semb).astype(BF16)
        push_ref[rows, WIDTH:] = (mm(place, meta) + jnp.concatenate([pieces] * (count // 64), axis=0)).astype(BF16)
    out.wait()


def prepare(emb, src_row, owner, dst_row, ec, neg_ids):
    return pl.pallas_call(
        prepare_kernel,
        in_specs=[HBM] * 6,
        out_specs=[VMEM, HBM, VMEM],
        out_shape=[
            pltpu.VMEM((SLOTS, WIDE), BF16),
            pltpu.HBM((EDGES, WIDTH), BF16),
            jax.ShapeDtypeStruct((1, EDGES), jnp.int32),
        ],
        scratch_shapes=[
            pltpu.VMEM((ROWS, WIDTH), BF16),
            pltpu.VMEM((1, EDGES), jnp.int32),
            pltpu.VMEM((1, EDGES), jnp.int32),
            pltpu.VMEM((1, EDGES), jnp.int32),
            pltpu.VMEM((1, DEVICES), jnp.int32),
            pltpu.SMEM((NEG,), jnp.int32),
            pltpu.VMEM((EDGES, WIDTH), BF16),
            pltpu.SemaphoreType.DMA((7,)),
        ],
        compiler_params=pltpu.CompilerParams(vmem_limit_bytes=24 * MIB),
        name="prepare",
    )(*in_hbm(emb, src_row, owner, dst_row, ec, neg_ids))


def pick_kernel(recv_ref, out_ref):
    told = recv_ref[:, WIDTH:].astype(F32)
    piece = jnp.sum(told.reshape(DEVICES, CAP, LANES), axis=0)
    part = lax.axis_index("c") * 4 + lax.axis_index("x")
    high = iota((NEG, LANES), 1) >= LANES // 2
    for i in range(4):
        low = jnp.logical_and(jnp.logical_not(high), part == 2 * i)
        tile = jnp.where(low, pltpu.roll(piece, LANES // 2, 1), 0.0)
        tile = jnp.where(jnp.logical_and(high, part == 2 * i + 1), piece, tile)
        out_ref[:, LANES * i:LANES * (i + 1)] = tile


def pick(recv):
    return pl.pallas_call(
        pick_kernel,
        in_specs=[VMEM],
        out_specs=VMEM,
        out_shape=jax.ShapeDtypeStruct((NEG, WIDTH), F32),
        compiler_params=pltpu.CompilerParams(vmem_limit_bytes=16 * MIB),
        name="pick",
    )(recv)


def stack(parts):
    return jnp.concatenate(parts, axis=0) if len(parts) > 1 else parts[0]


def decode_parts(xs, heads, w1, w2, wsb, wsr, g1_ref, g2_ref, ready=None, summed=None):
    first = [gate(mm(x, w1)) for x in xs]
    a1s = [a.astype(BF16) for a, _ in first]
    second = [gate(mm(a, w2)) for a in a1s]
    dz2s = []
    for (a2, slope), head in zip(second, heads):
        ds = wide(head(mm(a2.astype(BF16), wsb), a2))
        dz2s.append((ds * (wsr * slope)).astype(BF16))
    dz1s = [(mm_nt(dz2, w2) * slope).astype(BF16) for dz2, (_, slope) in zip(dz2s, first)]
    if ready is not None:
        ready()
    g2_ref[...] += mm_tn(stack(a1s), stack(dz2s))
    g1_ref[...] += mm_tn(stack(xs), stack(dz1s))
    if summed is not None:
        summed()
    return [mm_nt(dz1, w1) for dz1 in dz1s]


def scores(ws_ref):
    ws = ws_ref[...].astype(F32)
    return jnp.transpose(jnp.broadcast_to(ws, (LANES, WIDTH))).astype(BF16), ws * 0.5


def positive_kernel(recv_ref, emb_ref, w1_hbm, w2_hbm, ws_ref, ec_ref,
                    ret_ref, gdst_hbm, row_ref, g1_hbm, g2_hbm, gs_ref, loss_ref,
                    w1_ref, w2_ref, gdst_ref, g1_ref, g2_ref, sems, out_sems):
    ins = [pltpu.make_async_copy(a, b, sems.at[i]) for i, (a, b) in enumerate([(w1_hbm, w1_ref), (w2_hbm, w2_ref)])]
    for copy in ins:
        copy.start()
    _, total = counts(ec_ref)
    wsb, wsr = scores(ws_ref)
    g1_ref[...] = jnp.zeros_like(g1_ref)
    g2_ref[...] = jnp.zeros_like(g2_ref)
    gs_ref[...] = jnp.zeros_like(gs_ref)
    loss_ref[...] = jnp.zeros_like(loss_ref)
    spread = iota((LANES, 2 * LANES), 0)
    right = iota((LANES, 2 * LANES), 1) >= LANES
    table = jnp.where(
        right,
        jnp.where(spread == 2, 1.0, 0.0),
        jnp.where(spread == 0, 64.0, jnp.where(spread == 1, 1.0, 0.0)),
    ).astype(BF16)
    lane = iota((8, LANES), 1)
    sub = iota((8, LANES), 0)
    flag = jnp.where(jnp.logical_and(sub == 0, lane == 2), 1.0, 0.0).astype(BF16)
    taken = mm_nt(flag, recv_ref[:, WIDTH:WIDE])[0:1, :]
    taken = jnp.concatenate([taken[:, LANES * j:LANES * (j + 1)] for j in range(8)], axis=0)
    before = one(iota((LANES, LANES), 0) < iota((LANES, LANES), 1))
    place = mm(taken.astype(BF16), before)
    held = jnp.broadcast_to(jnp.sum(taken, axis=1, keepdims=True), (8, LANES))
    offset = jnp.zeros((8, LANES), F32)
    for j in range(7):
        offset = offset + jnp.where(sub > j, held[j:j + 1, :], 0.0)
    place = jnp.where(taken > 0.5, place + offset, -1.0).astype(jnp.int32)
    place = jnp.concatenate([place[j:j + 1, :] for j in range(8)], axis=1)
    place_col = column(place)
    half = SLOTS // 2
    rounds = jnp.where(jnp.sum(taken) > half, 2, 1)
    row_ref[...] = jnp.full(row_ref.shape, -1.0, F32)
    ret_ref[...] = jnp.zeros_like(ret_ref)

    def step(h, carry):
        rows = pl.ds(pl.multiple_of(h * half, half), half)
        chosen = one(iota((half, SLOTS), 0) + h * half == place)
        got = mm(chosen, recv_ref[...])
        src = got[:, 0:WIDTH]
        told = mm(got[:, WIDTH:].astype(BF16), table)
        live = told[:, LANES:]
        row = jnp.where(live > 0.5, told[:, :LANES], -1.0)
        row_ref[:, rows] = jnp.transpose(row)[0:8, :]
        dst = mm(onehot_rows(row.astype(jnp.int32), ROWS), emb_ref[...])

        def head(score, a2):
            loss_ref[...] += jnp.sum(live * softplus(-score), axis=0, keepdims=True) / total
            ds = -live * jax.nn.sigmoid(-score) / total
            gs_ref[...] += jnp.sum(wide(ds) * a2, axis=0, keepdims=True)
            return ds

        outs = [
            pltpu.make_async_copy(g1_ref, g1_hbm, out_sems.at[0]),
            pltpu.make_async_copy(g2_ref, g2_hbm, out_sems.at[1]),
            pltpu.make_async_copy(gdst_ref.at[rows, :], gdst_hbm.at[rows, :], out_sems.at[2]),
        ]

        def summed():
            for copy in outs[:2]:
                copy.start()

        @pl.when(h == 0)
        def _():
            for copy in ins:
                copy.wait()

        w1 = w1_ref[...] * BF16(0.5)
        w2 = w2_ref[...] * BF16(0.5)

        (dx,) = decode_parts([(src * dst).astype(BF16)], [head], w1, w2, wsb, wsr, g1_ref, g2_ref, None, summed)
        dx = dx * 2.0
        gdst_ref[rows, :] = (dx * src).astype(BF16)
        outs[2].start()
        back = mm(onehot_rows(place_col - h * half, half), (dx * dst).astype(BF16))
        ret_ref[...] = (ret_ref[...].astype(F32) + back).astype(BF16)
        for copy in outs:
            copy.wait()
        return carry

    lax.fori_loop(0, rounds, step, 0)


def positive(recv, emb, w1, w2, ws, ec):
    return pl.pallas_call(
        positive_kernel,
        in_specs=[VMEM, VMEM, HBM, HBM, VMEM, VMEM],
        out_specs=[VMEM, HBM, VMEM, HBM, HBM, VMEM, VMEM],
        out_shape=[
            pltpu.VMEM((SLOTS, WIDTH), BF16),
            pltpu.HBM((SLOTS, WIDTH), BF16),
            jax.ShapeDtypeStruct((8, SLOTS), F32),
            pltpu.HBM((WIDTH, WIDTH), F32),
            pltpu.HBM((WIDTH, WIDTH), F32),
            jax.ShapeDtypeStruct((1, WIDTH), F32),
            jax.ShapeDtypeStruct((1, LANES), F32),
        ],
        scratch_shapes=[
            pltpu.VMEM((WIDTH, WIDTH), BF16),
            pltpu.VMEM((WIDTH, WIDTH), BF16),
            pltpu.VMEM((SLOTS, WIDTH), BF16),
            pltpu.VMEM((WIDTH, WIDTH), F32),
            pltpu.VMEM((WIDTH, WIDTH), F32),
            pltpu.SemaphoreType.DMA((2,)),
            pltpu.SemaphoreType.DMA((3,)),
        ],
        compiler_params=pltpu.CompilerParams(vmem_limit_bytes=36 * MIB),
        cost_estimate=pl.CostEstimate(flops=6_000_000_000, bytes_accessed=12 * MIB, transcendentals=0),
        name="positive",
    )(recv, emb, *in_hbm(w1, w2), ws, ec)


def negative_kernel(semb_ref, neg_ref, w1_ref, w2_ref, ws_ref, ec_ref, g1_in, g2_in, gs_in, loss_in,
                    keep_hbm, send_ref, gsrc_hbm, extra_ref, gsrc_ref, g1_ref, g2_ref, gs_ref, loss_ref, gneg_ref,
                    sems):
    ins = [pltpu.make_async_copy(a, b, sems.at[i]) for i, (a, b) in enumerate([(g1_in, g1_ref), (g2_in, g2_ref)])]
    for copy in ins:
        copy.start()
    mine, total = counts(ec_ref)
    wsb, wsr = scores(ws_ref)
    gs_ref[...] = gs_in[...]
    loss_ref[...] = loss_in[...]
    gsrc_ref[...] = jnp.zeros_like(gsrc_ref)
    scale = 1.0 / (NEG * total)
    live = jnp.where(iota((EDGES, LANES), 0).astype(F32) < mine, scale, 0.0)

    def head(score, a2):
        loss_ref[...] += jnp.sum(live * softplus(score), axis=0, keepdims=True)
        ds = live * jax.nn.sigmoid(score)
        gs_ref[...] += jnp.sum(wide(ds) * a2, axis=0, keepdims=True)
        return ds

    w1 = w1_ref[...] * BF16(0.5)
    w2 = w2_ref[...] * BF16(0.5)

    def step(i, carry):
        src = semb_ref[...].astype(F32)
        ks = [4 * i + j for j in range(4)]
        negs = [neg_ref[pl.ds(k, 1), :] for k in ks]
        xs = [(src * n).astype(BF16) for n in negs]

        def ready():
            @pl.when(i == 0)
            def _():
                for copy in ins:
                    copy.wait()

        dxs = decode_parts(xs, [head] * 4, w1, w2, wsb, wsr, g1_ref, g2_ref, ready)
        gsrc = gsrc_ref[...]
        for k, n, dx in zip(ks, negs, dxs):
            gsrc = gsrc + dx * n
            gneg_ref[pl.ds(k, 1), :] = jnp.sum(dx * src, axis=0, keepdims=True)
        gsrc_ref[...] = gsrc
        return carry

    lax.fori_loop(0, NEG // 4, step, 0)
    out = pltpu.make_async_copy(gsrc_ref, gsrc_hbm, sems.at[2])
    out.start()
    loss = jnp.concatenate([loss_ref[...], jnp.zeros((1, WIDTH - LANES), F32)], axis=1)
    extra = jnp.concatenate([gneg_ref[...] * 2.0, gs_ref[...], loss, jnp.zeros((6, WIDTH), F32)], axis=0)
    extra_ref[...] = extra
    send_ref[WIDTH:, :] = extra
    core = lax.axis_index("c")
    for at, (kept, sent) in enumerate([(g1_ref, g2_ref), (g2_ref, g1_ref)]):
        @pl.when(core == at)
        def _():
            copy = pltpu.make_async_copy(kept, keep_hbm, sems.at[3])
            copy.start()
            send_ref[0:WIDTH, :] = sent[...]
            copy.wait()

    out.wait()


def negative(semb, negs, w1, w2, ws, ec, g1, g2, gs, loss):
    return pl.pallas_call(
        negative_kernel,
        in_specs=[VMEM] * 6 + [HBM] * 2 + [VMEM] * 2,
        out_specs=[HBM, VMEM, HBM, VMEM],
        out_shape=[
            pltpu.HBM((WIDTH, WIDTH), F32),
            jax.ShapeDtypeStruct((TALL, WIDTH), F32),
            pltpu.HBM((EDGES, WIDTH), F32),
            jax.ShapeDtypeStruct((TALL - WIDTH, WIDTH), F32),
        ],
        scratch_shapes=[pltpu.VMEM((WIDTH, WIDTH), F32)] * 3 + [
            pltpu.VMEM((1, WIDTH), F32),
            pltpu.VMEM((1, LANES), F32),
            pltpu.VMEM((NEG, WIDTH), F32),
            pltpu.SemaphoreType.DMA((4,)),
        ],
        compiler_params=pltpu.CompilerParams(vmem_limit_bytes=40 * MIB),
        cost_estimate=pl.CostEstimate(flops=20_000_000_000, bytes_accessed=8 * MIB, transcendentals=0),
        name="negative",
    )(semb, negs, w1, w2, ws, ec, *in_hbm(g1, g2), gs, loss)


def join_kernel(keep_hbm, got_ref, mine_ref, out_ref, keep_ref, sems):
    count = WIDTH // 4
    copies = []
    for q in range(4):
        rows = pl.ds(q * count, count)
        copies.append(pltpu.make_async_copy(keep_hbm.at[rows, :], keep_ref.at[rows, :], sems.at[q]))
        copies[q].start()
    extra = mine_ref[...] + got_ref[WIDTH:, :]
    tiles = []
    for k in range(NEG + 2):
        block = jnp.concatenate([extra[k:k + 1, LANES * j:LANES * (j + 1)] for j in range(4)], axis=0)
        high = block.astype(BF16).astype(F32)
        tiles += [high, block - high]
    tiles.append(jnp.zeros((WIDTH - 8 * (NEG + 2), LANES), F32))
    out_ref[:, WIDTH:] = stack(tiles).astype(BF16)
    for q in range(4):
        rows = pl.ds(q * count, count)
        copies[q].wait()
        out_ref[rows, 0:WIDTH] = (keep_ref[rows, :] + got_ref[rows, :]).astype(BF16)


def join(keep, got, mine):
    return pl.pallas_call(
        join_kernel,
        in_specs=[HBM, VMEM, VMEM],
        out_specs=VMEM,
        out_shape=jax.ShapeDtypeStruct((WIDTH, WIDE), BF16),
        scratch_shapes=[pltpu.VMEM((WIDTH, WIDTH), F32), pltpu.SemaphoreType.DMA((4,))],
        compiler_params=pltpu.CompilerParams(vmem_limit_bytes=16 * MIB),
        name="join",
    )(*in_hbm(keep), got, mine)


def block_of(node):
    local = node - lax.axis_index(AXES) * ROWS
    held = jnp.logical_and(local >= 0, local < ROWS)
    return held, jnp.where(held, local // 8 * 8, 0)


def scatter_kernel(gsrc_ref, back_ref, pos_ref, src_ref, gdst_ref, row_ref, neg_ref,
                   out_ref, near_ref, shi, slo, dst):
    block = out_ref.shape[0]

    @pl.when(pl.program_id(0) == 0)
    def _():
        placed = onehot_rows(column(pos_ref[...]), SLOTS)
        used = column(row_ref[0:1, :]) >= 0
        dst[...] = jnp.where(wide(used.astype(F32)) > 0.5, gdst_ref[...].astype(F32), 0.0).astype(BF16)
        shi[...], slo[...] = split(gsrc_ref[...] * 2.0 + mm(placed, back_ref[...]))
        near_ref[...] = jnp.zeros_like(near_ref)

    base = pl.program_id(0) * block
    mine = one(iota((block, EDGES), 0) + base == src_ref[...])
    theirs = one(iota((block, SLOTS), 0) + base == row_ref[0:1, :].astype(jnp.int32))
    out_ref[...] = (mm(mine, shi[...]) + mm(mine, slo[...])) + mm(theirs, dst[...])
    for k in range(NEG):
        held, at = block_of(neg_ref[k])

        @pl.when(jnp.logical_and(held, jnp.logical_and(at >= base, at < base + block)))
        def _():
            near_ref[k] = out_ref[pl.ds(pl.multiple_of(jnp.clip(at - base, 0, block - 8), 8), 8), :]


def scatter(gsrc, back, pos, src_row, gdst, rows, neg_ids):
    block = 512
    whole = lambda shape: pl.BlockSpec(shape, lambda i: (0, 0))
    return pl.pallas_call(
        scatter_kernel,
        grid=(ROWS // block,),
        in_specs=[
            whole((EDGES, WIDTH)), whole((SLOTS, WIDTH)), whole((1, EDGES)),
            whole((1, EDGES)), whole((SLOTS, WIDTH)), whole((8, SLOTS)), SMEM,
        ],
        out_specs=[pl.BlockSpec((block, WIDTH), lambda i: (i, 0)), pl.BlockSpec((NEG, 8, WIDTH), lambda i: (0, 0, 0))],
        out_shape=[jax.ShapeDtypeStruct((ROWS, WIDTH), F32), jax.ShapeDtypeStruct((NEG, 8, WIDTH), F32)],
        scratch_shapes=[
            pltpu.VMEM((EDGES, WIDTH), BF16), pltpu.VMEM((EDGES, WIDTH), BF16),
            pltpu.VMEM((SLOTS, WIDTH), BF16),
        ],
        compiler_params=pltpu.CompilerParams(vmem_limit_bytes=24 * MIB),
        cost_estimate=pl.CostEstimate(flops=7_000_000_000, bytes_accessed=10 * MIB, transcendentals=0),
        name="scatter",
    )(gsrc, back, pos, src_row, gdst, rows, neg_ids)


def total_kernel(parts_ref, out_ref):
    def step(i, acc):
        rows = pl.ds(pl.multiple_of(i * 64, 64), 64)
        part = parts_ref[rows, :].astype(F32)
        for j in range(8):
            acc = acc + part[8 * j:8 * j + 8, :]
        return acc

    acc = lax.fori_loop(0, GROUP // 8, step, jnp.zeros((CAP, WIDE), F32))
    extra = acc[:, WIDTH:]
    extra = extra[0:4, :] + extra[4:8, :]
    high = extra.astype(BF16).astype(F32)
    line = jnp.concatenate([acc[:, :WIDTH], jnp.concatenate([high, extra - high], axis=0)], axis=1)
    both = jnp.concatenate([line, line], axis=0).astype(BF16)

    def store(i, carry):
        out_ref[pl.ds(pl.multiple_of(i * 16, 16), 16), :] = both
        return carry

    lax.fori_loop(0, GROUP // 2, store, 0)


def total_up(parts):
    return pl.pallas_call(
        total_kernel,
        in_specs=[VMEM],
        out_specs=VMEM,
        out_shape=jax.ShapeDtypeStruct((WIDTH, WIDE), BF16),
        compiler_params=pltpu.CompilerParams(vmem_limit_bytes=16 * MIB),
        name="total_up",
    )(parts)


def sent_out(sums_ref, f_ref, out_hbm, sems):
    copies = []
    for h in range(4):
        rows = pl.ds(h * 128, 128)
        f_ref[rows, :] = sums_ref[rows, 0:WIDTH].astype(F32)
        copies.append(pltpu.make_async_copy(f_ref.at[rows, :], out_hbm.at[rows, :], sems.at[h]))
        copies[h].start()
    return copies


def own_kernel(sums_ref, neg_ref, near_ref, grads_in, g1_hbm, g2_hbm, gs_ref, loss_ref, grads_ref, half_ref, blocks, sems, out_sems):
    mine, bases = zip(*[block_of(neg_ref[k]) for k in range(NEG)])
    me = lax.axis_index(AXES)

    def put(k):
        rows = pl.ds(pl.multiple_of(bases[k], 8), 8)
        return pltpu.make_async_copy(blocks.at[k], grads_ref.at[rows, :], sems.at[k])

    extra = sums_ref[0:8 * (NEG + 2), WIDTH:].astype(F32)

    def line(k):
        block = extra[8 * k:8 * k + 4, :] + extra[8 * k + 4:8 * k + 8, :]
        return jnp.concatenate([block[j:j + 1, :] for j in range(4)], axis=1)

    gs_ref[...] = line(NEG)
    loss_ref[...] = line(NEG + 1)[:, 0:LANES]
    sub = iota((8, WIDTH), 0)
    for k in range(NEG):
        block = near_ref[k]
        for j in range(NEG):
            local = neg_ref[j] - me * ROWS
            hit = jnp.logical_and(mine[j], bases[j] == bases[k])
            at = jnp.where(hit, local - bases[k], -1)
            block = block + jnp.where(sub == at, line(j), 0.0)
        blocks[k] = block

        @pl.when(mine[k])
        def _():
            put(k).start()

    core = lax.axis_index("c")
    for at, g_hbm in enumerate([g1_hbm, g2_hbm]):
        @pl.when(core == at)
        def _():
            sent_out(sums_ref, half_ref, g_hbm, out_sems.at[at])

    for k in range(NEG):
        @pl.when(mine[k])
        def _():
            put(k).wait()

    for at, g_hbm in enumerate([g1_hbm, g2_hbm]):
        @pl.when(core == at)
        def _():
            for h in range(4):
                rows = pl.ds(h * 128, 128)
                pltpu.make_async_copy(half_ref.at[rows, :], g_hbm.at[rows, :], out_sems.at[at, h]).wait()


def finish_own(sums, neg_ids, near, grads):
    return pl.pallas_call(
        own_kernel,
        in_specs=[VMEM, SMEM, VMEM, pl.BlockSpec(memory_space=pl.ANY)],
        out_specs=[HBM, HBM, VMEM, VMEM, pl.BlockSpec(memory_space=pl.ANY)],
        out_shape=[
            pltpu.HBM((WIDTH, WIDTH), F32),
            pltpu.HBM((WIDTH, WIDTH), F32),
            jax.ShapeDtypeStruct((1, WIDTH), F32),
            jax.ShapeDtypeStruct((1, LANES), F32),
            jax.ShapeDtypeStruct((ROWS, WIDTH), F32),
        ],
        input_output_aliases={3: 4},
        scratch_shapes=[
            pltpu.VMEM((WIDTH, WIDTH), F32),
            pltpu.VMEM((NEG, 8, WIDTH), F32),
            pltpu.SemaphoreType.DMA((NEG,)),
            pltpu.SemaphoreType.DMA((2, 4)),
        ],
        compiler_params=pltpu.CompilerParams(vmem_limit_bytes=16 * MIB),
        cost_estimate=pl.CostEstimate(flops=1_000_000, bytes_accessed=2 * MIB, transcendentals=0),
        name="finish_own",
    )(sums, neg_ids, near, grads)


def other_kernel(other_ref, g1_in, g2_in, g1_hbm, g2_hbm, rest_ref, sems):
    core = lax.axis_index("c")
    for at, g_hbm in enumerate([g2_hbm, g1_hbm]):
        @pl.when(core == at)
        def _():
            for copy in sent_out(other_ref, rest_ref, g_hbm, sems.at[at]):
                copy.wait()


def finish_other(other, g1, g2):
    return pl.pallas_call(
        other_kernel,
        in_specs=[VMEM, HBM, HBM],
        out_specs=[HBM, HBM],
        out_shape=[pltpu.HBM((WIDTH, WIDTH), F32)] * 2,
        input_output_aliases={1: 0, 2: 1},
        scratch_shapes=[pltpu.VMEM((WIDTH, WIDTH), F32), pltpu.SemaphoreType.DMA((2, 4))],
        compiler_params=pltpu.CompilerParams(vmem_limit_bytes=16 * MIB),
        name="finish_other",
    )(other, *in_hbm(g1, g2))


def exchange(rows, axes):
    parts = rows.reshape(-1, CAP, rows.shape[1])
    out = lax.all_to_all(parts, axes, split_axis=0, concat_axis=0, tiled=True)
    return out.reshape(rows.shape)


def swap(rows):
    return lax.ppermute(rows, "c", [(0, 1), (1, 0)])


def complete(rows):
    rows = rows + swap(rows)
    got = [lax.ppermute(rows, "x", [(i, (i + by) % 4) for i in range(4)]) for by in (1, 2, 3)]
    return (rows + got[0]) + (got[1] + got[2])


def body(embeddings, w_first, w_second, w_score, src_row, dst_owner, dst_row, edge_count, neg_ids):
    ec = edge_count.reshape(1, DEVICES)
    ws = w_score.reshape(1, WIDTH)
    src_row = src_row.reshape(1, EDGES)
    push, semb, pos = prepare(
        embeddings, src_row, dst_owner.reshape(1, EDGES), dst_row.reshape(1, EDGES), ec, neg_ids
    )
    recv = exchange(push, AXES)
    negs = complete(pick(recv))
    ret, gdst, rows, g1, g2, gs, loss = positive(recv, embeddings, w_first, w_second, ws, ec)
    back = exchange(ret, AXES)
    keep, send, gsrc, extra = negative(semb, negs, w_first, w_second, ws, ec, g1, g2, gs, loss)
    send, back = lax.optimization_barrier((send, back))
    payload = join(keep, swap(send), extra)
    parts = exchange(payload, CHIPS)
    grads, near = scatter(gsrc, back, pos, src_row, gdst, rows, neg_ids)
    parts, grads = lax.optimization_barrier((parts, grads))
    sums = exchange(total_up(parts), CHIPS)
    other = swap(sums)
    g1, g2, gs, loss, grads = finish_own(sums, neg_ids, near, grads)
    g1, g2 = finish_other(other, g1, g2)
    return grads, g1, g2, gs.reshape(WIDTH), loss[0, 0]


def solution(mesh):
    mesh = Mesh(mesh.devices.reshape(4, 4, 2, 4), AXES)
    in_specs = (
        P(AXES, None), P(), P(), P(), P(AXES), P(AXES, None), P(AXES), P(), P(),
    )
    out_specs = (P(AXES, None), P(), P(), P(), P())
    return jax.shard_map(body, mesh=mesh, in_specs=in_specs, out_specs=out_specs, check_vma=False)
```

```python
import jax
import jax.numpy as jnp
from jax import lax
from jax.experimental import pallas as pl
from jax.experimental.pallas import tpu as pltpu
from jax.sharding import Mesh, PartitionSpec as P

F32 = jnp.float32
BF16 = jnp.bfloat16
AXES = ("z", "y", "c", "x")
CHIPS = ("z", "y", "x")
VMEM = pl.BlockSpec(memory_space=pltpu.VMEM)
SMEM = pl.BlockSpec(memory_space=pltpu.SMEM)
HBM = pl.BlockSpec(memory_space=pltpu.HBM)
MIB = 1 << 20


def in_hbm(*arrays):
    return tuple(pltpu.with_memory_space_constraint(a, pltpu.HBM) for a in arrays)


DEVICES = 128
GROUP = 64
ROWS = 2048
EDGES = 512
WIDTH = 512
NEG = 8
CAP = 8
SLOTS = DEVICES * CAP
LANES = 128
WIDE = WIDTH + LANES
TALL = WIDTH + 16


def mm(a, b):
    return jnp.dot(a, b, preferred_element_type=F32)


def mm_nt(a, b):
    return lax.dot_general(a, b, (((1,), (1,)), ((), ())), preferred_element_type=F32)


def mm_tn(a, b):
    return lax.dot_general(a, b, (((0,), (0,)), ((), ())), preferred_element_type=F32)


def wide(value):
    return jnp.concatenate([value] * (WIDTH // LANES), axis=1)


def iota(shape, dim):
    return lax.broadcasted_iota(jnp.int32, shape, dim)


def one(mask):
    return jnp.where(mask, 1.0, 0.0).astype(BF16)


def column(row):
    return jnp.transpose(jnp.broadcast_to(row.astype(F32), (LANES, row.shape[1]))).astype(jnp.int32)


def onehot_rows(col, count):
    lane = iota(col.shape, 1)
    return jnp.concatenate([one(col == lane + LANES * j) for j in range(count // LANES)], axis=1)


def split(value):
    high = value.astype(BF16)
    return high, (value - high.astype(F32)).astype(BF16)


def softplus(value):
    return jnp.maximum(value, 0.0) + jnp.log1p(jnp.exp(-jnp.abs(value)))


def gate(half):
    t = jnp.tanh(half)
    m = half * t
    return half + m, (1.0 + t) * (1.0 + (half - m))


def counts(ec_ref):
    me = lax.axis_index(AXES)
    ec = ec_ref[...]
    mine = jnp.sum(jnp.where(iota(ec.shape, 1) == me, ec, 0).astype(F32), axis=1, keepdims=True)
    return mine, jnp.sum(ec.astype(F32), axis=1, keepdims=True)


def prepare_kernel(emb_hbm, src_hbm, owner_hbm, dst_hbm, ec_hbm, neg_hbm, push_ref, semb_hbm, pos_ref,
                   emb_ref, src_ref, owner_ref, dst_ref, ec_ref, neg_ref, semb_ref, sems):
    pairs = [(neg_hbm, neg_ref), (ec_hbm, ec_ref), (owner_hbm, owner_ref), (src_hbm, src_ref),
             (dst_hbm, dst_ref), (emb_hbm, emb_ref)]
    copies = [pltpu.make_async_copy(a, b, sems.at[i]) for i, (a, b) in enumerate(pairs)]
    for copy in copies:
        copy.start()
    for copy in copies[:-1]:
        copy.wait()
    me = lax.axis_index(AXES)
    mine, _ = counts(ec_ref)
    live = iota((1, EDGES), 1).astype(F32) < mine
    owner = jnp.where(live, owner_ref[...], -1)
    named = one(iota((DEVICES, EDGES), 0) == owner)
    before = one(iota((EDGES, EDGES), 0) < iota((EDGES, EDGES), 1))
    rank = jnp.sum(mm(named, before) * named.astype(F32), axis=0, keepdims=True)
    pos = jnp.where(live, owner * CAP + rank.astype(jnp.int32), -1)
    pos_ref[...] = pos
    row = column(dst_ref[...])
    lane = iota((EDGES, LANES), 1)
    meta = jnp.where(lane == 0, row // 64, jnp.where(lane == 1, row % 64, jnp.where(lane == 2, 1, 0)))
    meta = meta.astype(F32).astype(BF16)
    sub = iota((2 * NEG, LANES), 0)
    local = jnp.full((2 * NEG, LANES), -1, jnp.int32)
    for k in range(NEG):
        local = jnp.where(sub == k, neg_ref[k] - me * ROWS, local)
    chosen = onehot_rows(jnp.concatenate([column(src_ref[...]), local], axis=0), ROWS)
    copies[-1].wait()
    emb = emb_ref[...]
    found = mm(chosen, emb)
    semb = found[0:EDGES, :].astype(BF16)
    semb_ref[...] = semb
    out = pltpu.make_async_copy(semb_ref, semb_hbm, sems.at[6])
    out.start()
    offers = found[EDGES:EDGES + NEG, :]
    high = iota((NEG, LANES), 1) >= LANES // 2
    pieces = []
    for q in range(4):
        tile = offers[:, LANES * q:LANES * (q + 1)]
        pieces += [jnp.where(high, pltpu.roll(tile, LANES // 2, 1), 0.0), jnp.where(high, tile, 0.0)]
    pieces = jnp.concatenate(pieces, axis=0)
    count = SLOTS // 4
    for q in range(4):
        rows = pl.ds(q * count, count)
        place = one(iota((count, EDGES), 0) + q * count == pos)
        push_ref[rows, 0:WIDTH] = mm(place, semb).astype(BF16)
        push_ref[rows, WIDTH:] = (mm(place, meta) + jnp.concatenate([pieces] * (count // 64), axis=0)).astype(BF16)
    out.wait()


def prepare(emb, src_row, owner, dst_row, ec, neg_ids):
    return pl.pallas_call(
        prepare_kernel,
        in_specs=[HBM] * 6,
        out_specs=[VMEM, HBM, VMEM],
        out_shape=[
            pltpu.VMEM((SLOTS, WIDE), BF16),
            pltpu.HBM((EDGES, WIDTH), BF16),
            jax.ShapeDtypeStruct((1, EDGES), jnp.int32),
        ],
        scratch_shapes=[
            pltpu.VMEM((ROWS, WIDTH), BF16),
            pltpu.VMEM((1, EDGES), jnp.int32),
            pltpu.VMEM((1, EDGES), jnp.int32),
            pltpu.VMEM((1, EDGES), jnp.int32),
            pltpu.VMEM((1, DEVICES), jnp.int32),
            pltpu.SMEM((NEG,), jnp.int32),
            pltpu.VMEM((EDGES, WIDTH), BF16),
            pltpu.SemaphoreType.DMA((7,)),
        ],
        compiler_params=pltpu.CompilerParams(vmem_limit_bytes=24 * MIB),
        name="prepare",
    )(*in_hbm(emb, src_row, owner, dst_row, ec, neg_ids))


def pick_kernel(recv_ref, out_ref):
    told = recv_ref[:, WIDTH:].astype(F32)
    piece = jnp.sum(told.reshape(DEVICES, CAP, LANES), axis=0)
    part = lax.axis_index("c") * 4 + lax.axis_index("x")
    high = iota((NEG, LANES), 1) >= LANES // 2
    for i in range(4):
        low = jnp.logical_and(jnp.logical_not(high), part == 2 * i)
        tile = jnp.where(low, pltpu.roll(piece, LANES // 2, 1), 0.0)
        tile = jnp.where(jnp.logical_and(high, part == 2 * i + 1), piece, tile)
        out_ref[:, LANES * i:LANES * (i + 1)] = tile


def pick(recv):
    return pl.pallas_call(
        pick_kernel,
        in_specs=[VMEM],
        out_specs=VMEM,
        out_shape=jax.ShapeDtypeStruct((NEG, WIDTH), F32),
        compiler_params=pltpu.CompilerParams(vmem_limit_bytes=16 * MIB),
        name="pick",
    )(recv)


def stack(parts):
    return jnp.concatenate(parts, axis=0) if len(parts) > 1 else parts[0]


def decode_parts(xs, heads, w1, w2, wsb, wsr, g1_ref, g2_ref, ready=None, summed=None):
    first = [gate(mm(x, w1)) for x in xs]
    a1s = [a.astype(BF16) for a, _ in first]
    second = [gate(mm(a, w2)) for a in a1s]
    dz2s = []
    for (a2, slope), head in zip(second, heads):
        ds = wide(head(mm(a2.astype(BF16), wsb), a2))
        dz2s.append((ds * (wsr * slope)).astype(BF16))
    dz1s = [(mm_nt(dz2, w2) * slope).astype(BF16) for dz2, (_, slope) in zip(dz2s, first)]
    if ready is not None:
        ready()
    g2_ref[...] += mm_tn(stack(a1s), stack(dz2s))
    g1_ref[...] += mm_tn(stack(xs), stack(dz1s))
    if summed is not None:
        summed()
    return [mm_nt(dz1, w1) for dz1 in dz1s]


def scores(ws_ref):
    ws = ws_ref[...].astype(F32)
    return jnp.transpose(jnp.broadcast_to(ws, (LANES, WIDTH))).astype(BF16), ws * 0.5


def positive_kernel(recv_ref, emb_ref, w1_hbm, w2_hbm, ws_ref, ec_ref,
                    ret_ref, gdst_hbm, row_ref, g1_hbm, g2_hbm, gs_ref, loss_ref,
                    w1_ref, w2_ref, gdst_ref, g1_ref, g2_ref, sems, out_sems):
    ins = [pltpu.make_async_copy(a, b, sems.at[i]) for i, (a, b) in enumerate([(w1_hbm, w1_ref), (w2_hbm, w2_ref)])]
    for copy in ins:
        copy.start()
    _, total = counts(ec_ref)
    wsb, wsr = scores(ws_ref)
    g1_ref[...] = jnp.zeros_like(g1_ref)
    g2_ref[...] = jnp.zeros_like(g2_ref)
    gs_ref[...] = jnp.zeros_like(gs_ref)
    loss_ref[...] = jnp.zeros_like(loss_ref)
    spread = iota((LANES, 2 * LANES), 0)
    right = iota((LANES, 2 * LANES), 1) >= LANES
    table = jnp.where(
        right,
        jnp.where(spread == 2, 1.0, 0.0),
        jnp.where(spread == 0, 64.0, jnp.where(spread == 1, 1.0, 0.0)),
    ).astype(BF16)
    lane = iota((8, LANES), 1)
    sub = iota((8, LANES), 0)
    flag = jnp.where(jnp.logical_and(sub == 0, lane == 2), 1.0, 0.0).astype(BF16)
    taken = mm_nt(flag, recv_ref[:, WIDTH:WIDE])[0:1, :]
    taken = jnp.concatenate([taken[:, LANES * j:LANES * (j + 1)] for j in range(8)], axis=0)
    before = one(iota((LANES, LANES), 0) < iota((LANES, LANES), 1))
    place = mm(taken.astype(BF16), before)
    held = jnp.broadcast_to(jnp.sum(taken, axis=1, keepdims=True), (8, LANES))
    offset = jnp.zeros((8, LANES), F32)
    for j in range(7):
        offset = offset + jnp.where(sub > j, held[j:j + 1, :], 0.0)
    place = jnp.where(taken > 0.5, place + offset, -1.0).astype(jnp.int32)
    place = jnp.concatenate([place[j:j + 1, :] for j in range(8)], axis=1)
    place_col = column(place)
    half = SLOTS // 2
    rounds = jnp.where(jnp.sum(taken) > half, 2, 1)
    row_ref[...] = jnp.full(row_ref.shape, -1.0, F32)
    ret_ref[...] = jnp.zeros_like(ret_ref)

    def step(h, carry):
        rows = pl.ds(pl.multiple_of(h * half, half), half)
        chosen = one(iota((half, SLOTS), 0) + h * half == place)
        got = mm(chosen, recv_ref[...])
        src = got[:, 0:WIDTH]
        told = mm(got[:, WIDTH:].astype(BF16), table)
        live = told[:, LANES:]
        row = jnp.where(live > 0.5, told[:, :LANES], -1.0)
        row_ref[:, rows] = jnp.transpose(row)[0:8, :]
        dst = mm(onehot_rows(row.astype(jnp.int32), ROWS), emb_ref[...])

        def head(score, a2):
            loss_ref[...] += jnp.sum(live * softplus(-score), axis=0, keepdims=True) / total
            ds = -live * jax.nn.sigmoid(-score) / total
            gs_ref[...] += jnp.sum(wide(ds) * a2, axis=0, keepdims=True)
            return ds

        outs = [
            pltpu.make_async_copy(g1_ref, g1_hbm, out_sems.at[0]),
            pltpu.make_async_copy(g2_ref, g2_hbm, out_sems.at[1]),
            pltpu.make_async_copy(gdst_ref.at[rows, :], gdst_hbm.at[rows, :], out_sems.at[2]),
        ]

        def summed():
            for copy in outs[:2]:
                copy.start()

        @pl.when(h == 0)
        def _():
            for copy in ins:
                copy.wait()

        w1 = w1_ref[...] * BF16(0.5)
        w2 = w2_ref[...] * BF16(0.5)

        (dx,) = decode_parts([(src * dst).astype(BF16)], [head], w1, w2, wsb, wsr, g1_ref, g2_ref, None, summed)
        dx = dx * 2.0
        gdst_ref[rows, :] = (dx * src).astype(BF16)
        outs[2].start()
        back = mm(onehot_rows(place_col - h * half, half), (dx * dst).astype(BF16))
        ret_ref[...] = (ret_ref[...].astype(F32) + back).astype(BF16)
        for copy in outs:
            copy.wait()
        return carry

    lax.fori_loop(0, rounds, step, 0)


def positive(recv, emb, w1, w2, ws, ec):
    return pl.pallas_call(
        positive_kernel,
        in_specs=[VMEM, VMEM, HBM, HBM, VMEM, VMEM],
        out_specs=[VMEM, HBM, VMEM, HBM, HBM, VMEM, VMEM],
        out_shape=[
            pltpu.VMEM((SLOTS, WIDTH), BF16),
            pltpu.HBM((SLOTS, WIDTH), BF16),
            jax.ShapeDtypeStruct((8, SLOTS), F32),
            pltpu.HBM((WIDTH, WIDTH), F32),
            pltpu.HBM((WIDTH, WIDTH), F32),
            jax.ShapeDtypeStruct((1, WIDTH), F32),
            jax.ShapeDtypeStruct((1, LANES), F32),
        ],
        scratch_shapes=[
            pltpu.VMEM((WIDTH, WIDTH), BF16),
            pltpu.VMEM((WIDTH, WIDTH), BF16),
            pltpu.VMEM((SLOTS, WIDTH), BF16),
            pltpu.VMEM((WIDTH, WIDTH), F32),
            pltpu.VMEM((WIDTH, WIDTH), F32),
            pltpu.SemaphoreType.DMA((2,)),
            pltpu.SemaphoreType.DMA((3,)),
        ],
        compiler_params=pltpu.CompilerParams(vmem_limit_bytes=36 * MIB),
        cost_estimate=pl.CostEstimate(flops=6_000_000_000, bytes_accessed=12 * MIB, transcendentals=0),
        name="positive",
    )(recv, emb, *in_hbm(w1, w2), ws, ec)


def negative_kernel(semb_hbm, neg_ref, w1_ref, w2_ref, ws_ref, ec_ref, g1_in, g2_in, gs_in, loss_in,
                    keep_hbm, send_ref, gsrc_hbm, extra_ref, gsrc_ref, g1_ref, g2_ref, gs_ref, loss_ref, gneg_ref,
                    semb_ref, sems):
    core = lax.axis_index("c")
    first = pltpu.make_async_copy(semb_hbm, semb_ref, sems.at[4])
    first.start()
    ins = [pltpu.make_async_copy(a, b, sems.at[i]) for i, (a, b) in enumerate([(g1_in, g1_ref), (g2_in, g2_ref)])]
    for copy in ins:
        copy.start()
    mine, total = counts(ec_ref)
    wsb, wsr = scores(ws_ref)
    gs_ref[...] = gs_in[...]
    loss_ref[...] = loss_in[...]
    gsrc_ref[...] = jnp.zeros_like(gsrc_ref)
    scale = 1.0 / (NEG * total)
    live = jnp.where(iota((EDGES, LANES), 0).astype(F32) < mine, scale, 0.0)

    def head(score, a2):
        loss_ref[...] += jnp.sum(live * softplus(score), axis=0, keepdims=True)
        ds = live * jax.nn.sigmoid(score)
        gs_ref[...] += jnp.sum(wide(ds) * a2, axis=0, keepdims=True)
        return ds

    w1 = w1_ref[...] * BF16(0.5)
    w2 = w2_ref[...] * BF16(0.5)

    first.wait()

    def step(i, carry):
        src = semb_ref[...].astype(F32)
        ks = [4 * i + j for j in range(4)]
        negs = [neg_ref[pl.ds(k, 1), :] for k in ks]
        xs = [(src * n).astype(BF16) for n in negs]

        def ready():
            @pl.when(i == 0)
            def _():
                for copy in ins:
                    copy.wait()

        def summed():
            for at, kept in enumerate([g1_ref, g2_ref]):
                @pl.when(jnp.logical_and(i == NEG // 4 - 1, core == at))
                def _():
                    pltpu.make_async_copy(kept, keep_hbm, sems.at[3]).start()

        dxs = decode_parts(xs, [head] * 4, w1, w2, wsb, wsr, g1_ref, g2_ref, ready, summed)
        gsrc = gsrc_ref[...]
        for k, n, dx in zip(ks, negs, dxs):
            gsrc = gsrc + dx * n
            gneg_ref[pl.ds(k, 1), :] = jnp.sum(dx * src, axis=0, keepdims=True)
        gsrc_ref[...] = gsrc
        return carry

    lax.fori_loop(0, NEG // 4, step, 0)
    out = pltpu.make_async_copy(gsrc_ref, gsrc_hbm, sems.at[2])
    out.start()
    loss = jnp.concatenate([loss_ref[...], jnp.zeros((1, WIDTH - LANES), F32)], axis=1)
    extra = jnp.concatenate([gneg_ref[...] * 2.0, gs_ref[...], loss, jnp.zeros((6, WIDTH), F32)], axis=0)
    extra_ref[...] = extra
    send_ref[WIDTH:, :] = extra
    for at, (kept, sent) in enumerate([(g1_ref, g2_ref), (g2_ref, g1_ref)]):
        @pl.when(core == at)
        def _():
            send_ref[0:WIDTH, :] = sent[...]
            pltpu.make_async_copy(kept, keep_hbm, sems.at[3]).wait()

    out.wait()


def negative(semb, negs, w1, w2, ws, ec, g1, g2, gs, loss):
    return pl.pallas_call(
        negative_kernel,
        in_specs=[HBM] + [VMEM] * 5 + [HBM] * 2 + [VMEM] * 2,
        out_specs=[HBM, VMEM, HBM, VMEM],
        out_shape=[
            pltpu.HBM((WIDTH, WIDTH), F32),
            jax.ShapeDtypeStruct((TALL, WIDTH), F32),
            pltpu.HBM((EDGES, WIDTH), F32),
            jax.ShapeDtypeStruct((TALL - WIDTH, WIDTH), F32),
        ],
        scratch_shapes=[pltpu.VMEM((WIDTH, WIDTH), F32)] * 3 + [
            pltpu.VMEM((1, WIDTH), F32),
            pltpu.VMEM((1, LANES), F32),
            pltpu.VMEM((NEG, WIDTH), F32),
            pltpu.VMEM((EDGES, WIDTH), BF16),
            pltpu.SemaphoreType.DMA((5,)),
        ],
        compiler_params=pltpu.CompilerParams(vmem_limit_bytes=40 * MIB),
        cost_estimate=pl.CostEstimate(flops=20_000_000_000, bytes_accessed=8 * MIB, transcendentals=0),
        name="negative",
    )(*in_hbm(semb), negs, w1, w2, ws, ec, *in_hbm(g1, g2), gs, loss)


def join_kernel(keep_hbm, got_ref, mine_ref, out_ref, keep_ref, sems):
    count = WIDTH // 4
    copies = []
    for q in range(4):
        rows = pl.ds(q * count, count)
        copies.append(pltpu.make_async_copy(keep_hbm.at[rows, :], keep_ref.at[rows, :], sems.at[q]))
        copies[q].start()
    extra = mine_ref[...] + got_ref[WIDTH:, :]
    tiles = []
    for k in range(NEG + 2):
        block = jnp.concatenate([extra[k:k + 1, LANES * j:LANES * (j + 1)] for j in range(4)], axis=0)
        high = block.astype(BF16).astype(F32)
        tiles += [high, block - high]
    tiles.append(jnp.zeros((WIDTH - 8 * (NEG + 2), LANES), F32))
    out_ref[:, WIDTH:] = stack(tiles).astype(BF16)
    for q in range(4):
        rows = pl.ds(q * count, count)
        copies[q].wait()
        out_ref[rows, 0:WIDTH] = (keep_ref[rows, :] + got_ref[rows, :]).astype(BF16)


def join(keep, got, mine):
    return pl.pallas_call(
        join_kernel,
        in_specs=[HBM, VMEM, VMEM],
        out_specs=VMEM,
        out_shape=jax.ShapeDtypeStruct((WIDTH, WIDE), BF16),
        scratch_shapes=[pltpu.VMEM((WIDTH, WIDTH), F32), pltpu.SemaphoreType.DMA((4,))],
        compiler_params=pltpu.CompilerParams(vmem_limit_bytes=16 * MIB),
        name="join",
    )(*in_hbm(keep), got, mine)


def block_of(node):
    local = node - lax.axis_index(AXES) * ROWS
    held = jnp.logical_and(local >= 0, local < ROWS)
    return held, jnp.where(held, local // 8 * 8, 0)


def scatter_kernel(gsrc_ref, back_ref, pos_ref, src_ref, gdst_ref, row_ref, neg_ref,
                   out_ref, near_ref, shi, slo, dst):
    block = out_ref.shape[0]

    @pl.when(pl.program_id(0) == 0)
    def _():
        placed = onehot_rows(column(pos_ref[...]), SLOTS)
        used = column(row_ref[0:1, :]) >= 0
        dst[...] = jnp.where(wide(used.astype(F32)) > 0.5, gdst_ref[...].astype(F32), 0.0).astype(BF16)
        shi[...], slo[...] = split(gsrc_ref[...] * 2.0 + mm(placed, back_ref[...]))
        near_ref[...] = jnp.zeros_like(near_ref)

    base = pl.program_id(0) * block
    mine = one(iota((block, EDGES), 0) + base == src_ref[...])
    theirs = one(iota((block, SLOTS), 0) + base == row_ref[0:1, :].astype(jnp.int32))
    out_ref[...] = (mm(mine, shi[...]) + mm(mine, slo[...])) + mm(theirs, dst[...])
    for k in range(NEG):
        held, at = block_of(neg_ref[k])

        @pl.when(jnp.logical_and(held, jnp.logical_and(at >= base, at < base + block)))
        def _():
            near_ref[k] = out_ref[pl.ds(pl.multiple_of(jnp.clip(at - base, 0, block - 8), 8), 8), :]


def scatter(gsrc, back, pos, src_row, gdst, rows, neg_ids):
    block = 512
    whole = lambda shape: pl.BlockSpec(shape, lambda i: (0, 0))
    return pl.pallas_call(
        scatter_kernel,
        grid=(ROWS // block,),
        in_specs=[
            whole((EDGES, WIDTH)), whole((SLOTS, WIDTH)), whole((1, EDGES)),
            whole((1, EDGES)), whole((SLOTS, WIDTH)), whole((8, SLOTS)), SMEM,
        ],
        out_specs=[pl.BlockSpec((block, WIDTH), lambda i: (i, 0)), pl.BlockSpec((NEG, 8, WIDTH), lambda i: (0, 0, 0))],
        out_shape=[jax.ShapeDtypeStruct((ROWS, WIDTH), F32), jax.ShapeDtypeStruct((NEG, 8, WIDTH), F32)],
        scratch_shapes=[
            pltpu.VMEM((EDGES, WIDTH), BF16), pltpu.VMEM((EDGES, WIDTH), BF16),
            pltpu.VMEM((SLOTS, WIDTH), BF16),
        ],
        compiler_params=pltpu.CompilerParams(vmem_limit_bytes=24 * MIB),
        cost_estimate=pl.CostEstimate(flops=7_000_000_000, bytes_accessed=10 * MIB, transcendentals=0),
        name="scatter",
    )(gsrc, back, pos, src_row, gdst, rows, neg_ids)


def total_kernel(parts_ref, out_ref):
    def step(i, acc):
        rows = pl.ds(pl.multiple_of(i * 64, 64), 64)
        part = parts_ref[rows, :].astype(F32)
        for j in range(8):
            acc = acc + part[8 * j:8 * j + 8, :]
        return acc

    acc = lax.fori_loop(0, GROUP // 8, step, jnp.zeros((CAP, WIDE), F32))
    extra = acc[:, WIDTH:]
    extra = extra[0:4, :] + extra[4:8, :]
    high = extra.astype(BF16).astype(F32)
    line = jnp.concatenate([acc[:, :WIDTH], jnp.concatenate([high, extra - high], axis=0)], axis=1)
    both = jnp.concatenate([line, line], axis=0).astype(BF16)

    def store(i, carry):
        out_ref[pl.ds(pl.multiple_of(i * 16, 16), 16), :] = both
        return carry

    lax.fori_loop(0, GROUP // 2, store, 0)


def total_up(parts):
    return pl.pallas_call(
        total_kernel,
        in_specs=[VMEM],
        out_specs=VMEM,
        out_shape=jax.ShapeDtypeStruct((WIDTH, WIDE), BF16),
        compiler_params=pltpu.CompilerParams(vmem_limit_bytes=16 * MIB),
        name="total_up",
    )(parts)


def sent_out(sums_ref, f_ref, out_hbm, sems):
    copies = []
    for h in range(4):
        rows = pl.ds(h * 128, 128)
        f_ref[rows, :] = sums_ref[rows, 0:WIDTH].astype(F32)
        copies.append(pltpu.make_async_copy(f_ref.at[rows, :], out_hbm.at[rows, :], sems.at[h]))
        copies[h].start()
    return copies


def own_kernel(sums_ref, neg_ref, near_ref, grads_in, g1_hbm, g2_hbm, gs_ref, loss_ref, grads_ref, half_ref, blocks, sems, out_sems):
    mine, bases = zip(*[block_of(neg_ref[k]) for k in range(NEG)])
    me = lax.axis_index(AXES)

    def put(k):
        rows = pl.ds(pl.multiple_of(bases[k], 8), 8)
        return pltpu.make_async_copy(blocks.at[k], grads_ref.at[rows, :], sems.at[k])

    extra = sums_ref[0:8 * (NEG + 2), WIDTH:].astype(F32)

    def line(k):
        block = extra[8 * k:8 * k + 4, :] + extra[8 * k + 4:8 * k + 8, :]
        return jnp.concatenate([block[j:j + 1, :] for j in range(4)], axis=1)

    gs_ref[...] = line(NEG)
    loss_ref[...] = line(NEG + 1)[:, 0:LANES]
    sub = iota((8, WIDTH), 0)
    for k in range(NEG):
        block = near_ref[k]
        for j in range(NEG):
            local = neg_ref[j] - me * ROWS
            hit = jnp.logical_and(mine[j], bases[j] == bases[k])
            at = jnp.where(hit, local - bases[k], -1)
            block = block + jnp.where(sub == at, line(j), 0.0)
        blocks[k] = block

        @pl.when(mine[k])
        def _():
            put(k).start()

    core = lax.axis_index("c")
    for at, g_hbm in enumerate([g1_hbm, g2_hbm]):
        @pl.when(core == at)
        def _():
            sent_out(sums_ref, half_ref, g_hbm, out_sems.at[at])

    for k in range(NEG):
        @pl.when(mine[k])
        def _():
            put(k).wait()

    for at, g_hbm in enumerate([g1_hbm, g2_hbm]):
        @pl.when(core == at)
        def _():
            for h in range(4):
                rows = pl.ds(h * 128, 128)
                pltpu.make_async_copy(half_ref.at[rows, :], g_hbm.at[rows, :], out_sems.at[at, h]).wait()


def finish_own(sums, neg_ids, near, grads):
    return pl.pallas_call(
        own_kernel,
        in_specs=[VMEM, SMEM, VMEM, pl.BlockSpec(memory_space=pl.ANY)],
        out_specs=[HBM, HBM, VMEM, VMEM, pl.BlockSpec(memory_space=pl.ANY)],
        out_shape=[
            pltpu.HBM((WIDTH, WIDTH), F32),
            pltpu.HBM((WIDTH, WIDTH), F32),
            jax.ShapeDtypeStruct((1, WIDTH), F32),
            jax.ShapeDtypeStruct((1, LANES), F32),
            jax.ShapeDtypeStruct((ROWS, WIDTH), F32),
        ],
        input_output_aliases={3: 4},
        scratch_shapes=[
            pltpu.VMEM((WIDTH, WIDTH), F32),
            pltpu.VMEM((NEG, 8, WIDTH), F32),
            pltpu.SemaphoreType.DMA((NEG,)),
            pltpu.SemaphoreType.DMA((2, 4)),
        ],
        compiler_params=pltpu.CompilerParams(vmem_limit_bytes=16 * MIB),
        cost_estimate=pl.CostEstimate(flops=1_000_000, bytes_accessed=2 * MIB, transcendentals=0),
        name="finish_own",
    )(sums, neg_ids, near, grads)


def other_kernel(other_ref, g1_in, g2_in, g1_hbm, g2_hbm, rest_ref, sems):
    core = lax.axis_index("c")
    for at, g_hbm in enumerate([g2_hbm, g1_hbm]):
        @pl.when(core == at)
        def _():
            for copy in sent_out(other_ref, rest_ref, g_hbm, sems.at[at]):
                copy.wait()


def finish_other(other, g1, g2):
    return pl.pallas_call(
        other_kernel,
        in_specs=[VMEM, HBM, HBM],
        out_specs=[HBM, HBM],
        out_shape=[pltpu.HBM((WIDTH, WIDTH), F32)] * 2,
        input_output_aliases={1: 0, 2: 1},
        scratch_shapes=[pltpu.VMEM((WIDTH, WIDTH), F32), pltpu.SemaphoreType.DMA((2, 4))],
        compiler_params=pltpu.CompilerParams(vmem_limit_bytes=16 * MIB),
        name="finish_other",
    )(other, *in_hbm(g1, g2))


def exchange(rows, axes):
    parts = rows.reshape(-1, CAP, rows.shape[1])
    out = lax.all_to_all(parts, axes, split_axis=0, concat_axis=0, tiled=True)
    return out.reshape(rows.shape)


def swap(rows):
    return lax.ppermute(rows, "c", [(0, 1), (1, 0)])


def complete(rows):
    rows = rows + swap(rows)
    got = [lax.ppermute(rows, "x", [(i, (i + by) % 4) for i in range(4)]) for by in (1, 2, 3)]
    return (rows + got[0]) + (got[1] + got[2])


def body(embeddings, w_first, w_second, w_score, src_row, dst_owner, dst_row, edge_count, neg_ids):
    ec = edge_count.reshape(1, DEVICES)
    ws = w_score.reshape(1, WIDTH)
    src_row = src_row.reshape(1, EDGES)
    push, semb, pos = prepare(
        embeddings, src_row, dst_owner.reshape(1, EDGES), dst_row.reshape(1, EDGES), ec, neg_ids
    )
    recv = exchange(push, AXES)
    negs = complete(pick(recv))
    ret, gdst, rows, g1, g2, gs, loss = positive(recv, embeddings, w_first, w_second, ws, ec)
    back = exchange(ret, AXES)
    keep, send, gsrc, extra = negative(semb, negs, w_first, w_second, ws, ec, g1, g2, gs, loss)
    send, back = lax.optimization_barrier((send, back))
    payload = join(keep, swap(send), extra)
    parts = exchange(payload, CHIPS)
    grads, near = scatter(gsrc, back, pos, src_row, gdst, rows, neg_ids)
    parts, grads = lax.optimization_barrier((parts, grads))
    sums = exchange(total_up(parts), CHIPS)
    other = swap(sums)
    g1, g2, gs, loss, grads = finish_own(sums, neg_ids, near, grads)
    g1, g2 = finish_other(other, g1, g2)
    return grads, g1, g2, gs.reshape(WIDTH), loss[0, 0]


def solution(mesh):
    mesh = Mesh(mesh.devices.reshape(4, 4, 2, 4), AXES)
    in_specs = (
        P(AXES, None), P(), P(), P(), P(AXES), P(AXES, None), P(AXES), P(), P(),
    )
    out_specs = (P(AXES, None), P(), P(), P(), P())
    return jax.shard_map(body, mesh=mesh, in_specs=in_specs, out_specs=out_specs, check_vma=False)
```

```python
import jax
import jax.numpy as jnp
from jax import lax
from jax.experimental import pallas as pl
from jax.experimental.pallas import tpu as pltpu
from jax.sharding import Mesh, PartitionSpec as P

F32 = jnp.float32
BF16 = jnp.bfloat16
AXES = ("z", "y", "c", "x")
CHIPS = ("z", "y", "x")
VMEM = pl.BlockSpec(memory_space=pltpu.VMEM)
SMEM = pl.BlockSpec(memory_space=pltpu.SMEM)
HBM = pl.BlockSpec(memory_space=pltpu.HBM)
MIB = 1 << 20


def in_hbm(*arrays):
    return tuple(pltpu.with_memory_space_constraint(a, pltpu.HBM) for a in arrays)


DEVICES = 128
GROUP = 64
ROWS = 2048
EDGES = 512
WIDTH = 512
NEG = 8
CAP = 8
SLOTS = DEVICES * CAP
LANES = 128
WIDE = WIDTH + LANES
TALL = WIDTH + 16


def mm(a, b):
    return jnp.dot(a, b, preferred_element_type=F32)


def mm_nt(a, b):
    return lax.dot_general(a, b, (((1,), (1,)), ((), ())), preferred_element_type=F32)


def mm_tn(a, b):
    return lax.dot_general(a, b, (((0,), (0,)), ((), ())), preferred_element_type=F32)


def wide(value):
    return jnp.concatenate([value] * (WIDTH // LANES), axis=1)


def iota(shape, dim):
    return lax.broadcasted_iota(jnp.int32, shape, dim)


def one(mask):
    return jnp.where(mask, 1.0, 0.0).astype(BF16)


def column(row):
    return jnp.transpose(jnp.broadcast_to(row.astype(F32), (LANES, row.shape[1]))).astype(jnp.int32)


def onehot_rows(col, count):
    lane = iota(col.shape, 1)
    return jnp.concatenate([one(col == lane + LANES * j) for j in range(count // LANES)], axis=1)


def split(value):
    high = value.astype(BF16)
    return high, (value - high.astype(F32)).astype(BF16)


def softplus(value):
    return jnp.maximum(value, 0.0) + jnp.log1p(jnp.exp(-jnp.abs(value)))


def gate(half):
    t = jnp.tanh(half)
    m = half * t
    return half + m, (1.0 + t) * (1.0 + (half - m))


def counts(ec_ref):
    me = lax.axis_index(AXES)
    ec = ec_ref[...]
    mine = jnp.sum(jnp.where(iota(ec.shape, 1) == me, ec, 0).astype(F32), axis=1, keepdims=True)
    return mine, jnp.sum(ec.astype(F32), axis=1, keepdims=True)


def prepare_kernel(emb_hbm, src_hbm, owner_hbm, dst_hbm, ec_hbm, neg_hbm, push_ref, semb_hbm, pos_ref,
                   emb_ref, src_ref, owner_ref, dst_ref, ec_ref, neg_ref, semb_ref, sems):
    pairs = [(neg_hbm, neg_ref), (ec_hbm, ec_ref), (owner_hbm, owner_ref), (src_hbm, src_ref),
             (dst_hbm, dst_ref), (emb_hbm, emb_ref)]
    copies = [pltpu.make_async_copy(a, b, sems.at[i]) for i, (a, b) in enumerate(pairs)]
    for copy in copies:
        copy.start()
    for copy in copies[:-1]:
        copy.wait()
    me = lax.axis_index(AXES)
    mine, _ = counts(ec_ref)
    live = iota((1, EDGES), 1).astype(F32) < mine
    owner = jnp.where(live, owner_ref[...], -1)
    named = one(iota((DEVICES, EDGES), 0) == owner)
    before = one(iota((EDGES, EDGES), 0) < iota((EDGES, EDGES), 1))
    rank = jnp.sum(mm(named, before) * named.astype(F32), axis=0, keepdims=True)
    pos = jnp.where(live, owner * CAP + rank.astype(jnp.int32), -1)
    pos_ref[...] = pos
    row = column(dst_ref[...])
    lane = iota((EDGES, LANES), 1)
    meta = jnp.where(lane == 0, row // 64, jnp.where(lane == 1, row % 64, jnp.where(lane == 2, 1, 0)))
    meta = meta.astype(F32).astype(BF16)
    sub = iota((2 * NEG, LANES), 0)
    local = jnp.full((2 * NEG, LANES), -1, jnp.int32)
    for k in range(NEG):
        local = jnp.where(sub == k, neg_ref[k] - me * ROWS, local)
    chosen = onehot_rows(jnp.concatenate([column(src_ref[...]), local], axis=0), ROWS)
    copies[-1].wait()
    emb = emb_ref[...]
    found = mm(chosen, emb)
    semb = found[0:EDGES, :].astype(BF16)
    semb_ref[...] = semb
    out = pltpu.make_async_copy(semb_ref, semb_hbm, sems.at[6])
    out.start()
    offers = found[EDGES:EDGES + NEG, :]
    high = iota((NEG, LANES), 1) >= LANES // 2
    pieces = []
    for q in range(4):
        tile = offers[:, LANES * q:LANES * (q + 1)]
        pieces += [jnp.where(high, pltpu.roll(tile, LANES // 2, 1), 0.0), jnp.where(high, tile, 0.0)]
    pieces = jnp.concatenate(pieces, axis=0)
    count = SLOTS // 4
    for q in range(4):
        rows = pl.ds(q * count, count)
        place = one(iota((count, EDGES), 0) + q * count == pos)
        push_ref[rows, 0:WIDTH] = mm(place, semb).astype(BF16)
        push_ref[rows, WIDTH:] = (mm(place, meta) + jnp.concatenate([pieces] * (count // 64), axis=0)).astype(BF16)
    out.wait()


def prepare(emb, src_row, owner, dst_row, ec, neg_ids):
    return pl.pallas_call(
        prepare_kernel,
        in_specs=[HBM] * 6,
        out_specs=[VMEM, HBM, VMEM],
        out_shape=[
            pltpu.VMEM((SLOTS, WIDE), BF16),
            pltpu.HBM((EDGES, WIDTH), BF16),
            jax.ShapeDtypeStruct((1, EDGES), jnp.int32),
        ],
        scratch_shapes=[
            pltpu.VMEM((ROWS, WIDTH), BF16),
            pltpu.VMEM((1, EDGES), jnp.int32),
            pltpu.VMEM((1, EDGES), jnp.int32),
            pltpu.VMEM((1, EDGES), jnp.int32),
            pltpu.VMEM((1, DEVICES), jnp.int32),
            pltpu.SMEM((NEG,), jnp.int32),
            pltpu.VMEM((EDGES, WIDTH), BF16),
            pltpu.SemaphoreType.DMA((7,)),
        ],
        compiler_params=pltpu.CompilerParams(vmem_limit_bytes=24 * MIB),
        name="prepare",
    )(*in_hbm(emb, src_row, owner, dst_row, ec, neg_ids))


def pick_kernel(recv_ref, out_ref):
    told = recv_ref[:, WIDTH:].astype(F32)
    piece = jnp.sum(told.reshape(DEVICES, CAP, LANES), axis=0)
    part = lax.axis_index("c") * 4 + lax.axis_index("x")
    high = iota((NEG, LANES), 1) >= LANES // 2
    for i in range(4):
        low = jnp.logical_and(jnp.logical_not(high), part == 2 * i)
        tile = jnp.where(low, pltpu.roll(piece, LANES // 2, 1), 0.0)
        tile = jnp.where(jnp.logical_and(high, part == 2 * i + 1), piece, tile)
        out_ref[:, LANES * i:LANES * (i + 1)] = tile


def pick(recv):
    return pl.pallas_call(
        pick_kernel,
        in_specs=[VMEM],
        out_specs=VMEM,
        out_shape=jax.ShapeDtypeStruct((NEG, WIDTH), F32),
        compiler_params=pltpu.CompilerParams(vmem_limit_bytes=16 * MIB),
        name="pick",
    )(recv)


def stack(parts):
    return jnp.concatenate(parts, axis=0) if len(parts) > 1 else parts[0]


def decode_parts(xs, heads, w1, w2, wsb, wsr, g1_ref, g2_ref, ready=None, summed=None):
    first = [gate(mm(x, w1)) for x in xs]
    a1s = [a.astype(BF16) for a, _ in first]
    second = [gate(mm(a, w2)) for a in a1s]
    dz2s = []
    for (a2, slope), head in zip(second, heads):
        ds = wide(head(mm(a2.astype(BF16), wsb), a2))
        dz2s.append((ds * (wsr * slope)).astype(BF16))
    dz1s = [(mm_nt(dz2, w2) * slope).astype(BF16) for dz2, (_, slope) in zip(dz2s, first)]
    if ready is not None:
        ready()
    g2_ref[...] += mm_tn(stack(a1s), stack(dz2s))
    g1_ref[...] += mm_tn(stack(xs), stack(dz1s))
    if summed is not None:
        summed()
    return [mm_nt(dz1, w1) for dz1 in dz1s]


def scores(ws_ref):
    ws = ws_ref[...].astype(F32)
    return jnp.transpose(jnp.broadcast_to(ws, (LANES, WIDTH))).astype(BF16), ws * 0.5


def positive_kernel(recv_ref, emb_ref, w1_hbm, w2_hbm, ws_ref, ec_ref,
                    ret_ref, gdst_hbm, row_ref, g1_hbm, g2_hbm, gs_ref, loss_ref,
                    w1_ref, w2_ref, gdst_ref, g1_ref, g2_ref, sems, out_sems):
    ins = [pltpu.make_async_copy(a, b, sems.at[i]) for i, (a, b) in enumerate([(w1_hbm, w1_ref), (w2_hbm, w2_ref)])]
    for copy in ins:
        copy.start()
    _, total = counts(ec_ref)
    wsb, wsr = scores(ws_ref)
    g1_ref[...] = jnp.zeros_like(g1_ref)
    g2_ref[...] = jnp.zeros_like(g2_ref)
    gs_ref[...] = jnp.zeros_like(gs_ref)
    loss_ref[...] = jnp.zeros_like(loss_ref)
    spread = iota((LANES, 2 * LANES), 0)
    right = iota((LANES, 2 * LANES), 1) >= LANES
    table = jnp.where(
        right,
        jnp.where(spread == 2, 1.0, 0.0),
        jnp.where(spread == 0, 64.0, jnp.where(spread == 1, 1.0, 0.0)),
    ).astype(BF16)
    lane = iota((8, LANES), 1)
    sub = iota((8, LANES), 0)
    flag = jnp.where(jnp.logical_and(sub == 0, lane == 2), 1.0, 0.0).astype(BF16)
    taken = mm_nt(flag, recv_ref[:, WIDTH:WIDE])[0:1, :]
    taken = jnp.concatenate([taken[:, LANES * j:LANES * (j + 1)] for j in range(8)], axis=0)
    before = one(iota((LANES, LANES), 0) < iota((LANES, LANES), 1))
    place = mm(taken.astype(BF16), before)
    held = jnp.broadcast_to(jnp.sum(taken, axis=1, keepdims=True), (8, LANES))
    offset = jnp.zeros((8, LANES), F32)
    for j in range(7):
        offset = offset + jnp.where(sub > j, held[j:j + 1, :], 0.0)
    place = jnp.where(taken > 0.5, place + offset, -1.0).astype(jnp.int32)
    place = jnp.concatenate([place[j:j + 1, :] for j in range(8)], axis=1)
    place_col = column(place)
    half = SLOTS // 2
    rounds = jnp.where(jnp.sum(taken) > half, 2, 1)
    row_ref[...] = jnp.full(row_ref.shape, -1.0, F32)
    ret_ref[...] = jnp.zeros_like(ret_ref)

    def step(h, carry):
        rows = pl.ds(pl.multiple_of(h * half, half), half)
        chosen = one(iota((half, SLOTS), 0) + h * half == place)
        got = mm(chosen, recv_ref[...])
        src = got[:, 0:WIDTH]
        told = mm(got[:, WIDTH:].astype(BF16), table)
        live = told[:, LANES:]
        row = jnp.where(live > 0.5, told[:, :LANES], -1.0)
        row_ref[:, rows] = jnp.transpose(row)[0:8, :]
        dst = mm(onehot_rows(row.astype(jnp.int32), ROWS), emb_ref[...])

        def head(score, a2):
            loss_ref[...] += jnp.sum(live * softplus(-score), axis=0, keepdims=True) / total
            ds = -live * jax.nn.sigmoid(-score) / total
            gs_ref[...] += jnp.sum(wide(ds) * a2, axis=0, keepdims=True)
            return ds

        outs = [
            pltpu.make_async_copy(g1_ref, g1_hbm, out_sems.at[0]),
            pltpu.make_async_copy(g2_ref, g2_hbm, out_sems.at[1]),
            pltpu.make_async_copy(gdst_ref.at[rows, :], gdst_hbm.at[rows, :], out_sems.at[2]),
        ]

        def summed():
            for copy in outs[:2]:
                copy.start()

        @pl.when(h == 0)
        def _():
            for copy in ins:
                copy.wait()

        w1 = w1_ref[...] * BF16(0.5)
        w2 = w2_ref[...] * BF16(0.5)

        (dx,) = decode_parts([(src * dst).astype(BF16)], [head], w1, w2, wsb, wsr, g1_ref, g2_ref, None, summed)
        dx = dx * 2.0
        gdst_ref[rows, :] = (dx * src).astype(BF16)
        outs[2].start()
        back = mm(onehot_rows(place_col - h * half, half), (dx * dst).astype(BF16))
        ret_ref[...] = (ret_ref[...].astype(F32) + back).astype(BF16)
        for copy in outs:
            copy.wait()
        return carry

    lax.fori_loop(0, rounds, step, 0)


def positive(recv, emb, w1, w2, ws, ec):
    return pl.pallas_call(
        positive_kernel,
        in_specs=[VMEM, VMEM, HBM, HBM, VMEM, VMEM],
        out_specs=[VMEM, HBM, VMEM, HBM, HBM, VMEM, VMEM],
        out_shape=[
            pltpu.VMEM((SLOTS, WIDTH), BF16),
            pltpu.HBM((SLOTS, WIDTH), BF16),
            jax.ShapeDtypeStruct((8, SLOTS), F32),
            pltpu.HBM((WIDTH, WIDTH), F32),
            pltpu.HBM((WIDTH, WIDTH), F32),
            jax.ShapeDtypeStruct((1, WIDTH), F32),
            jax.ShapeDtypeStruct((1, LANES), F32),
        ],
        scratch_shapes=[
            pltpu.VMEM((WIDTH, WIDTH), BF16),
            pltpu.VMEM((WIDTH, WIDTH), BF16),
            pltpu.VMEM((SLOTS, WIDTH), BF16),
            pltpu.VMEM((WIDTH, WIDTH), F32),
            pltpu.VMEM((WIDTH, WIDTH), F32),
            pltpu.SemaphoreType.DMA((2,)),
            pltpu.SemaphoreType.DMA((3,)),
        ],
        compiler_params=pltpu.CompilerParams(vmem_limit_bytes=36 * MIB),
        cost_estimate=pl.CostEstimate(flops=6_000_000_000, bytes_accessed=12 * MIB, transcendentals=0),
        name="positive",
    )(recv, emb, *in_hbm(w1, w2), ws, ec)


def negative_kernel(semb_hbm, neg_ref, w1_ref, w2_ref, ws_ref, ec_ref, g1_in, g2_in, gs_in, loss_in,
                    keep_hbm, send_ref, gsrc_hbm, extra_ref, gsrc_ref, g1_ref, g2_ref, gs_ref, loss_ref, gneg_ref,
                    semb_ref, sems):
    core = lax.axis_index("c")
    first = pltpu.make_async_copy(semb_hbm, semb_ref, sems.at[4])
    first.start()
    ins = [pltpu.make_async_copy(a, b, sems.at[i]) for i, (a, b) in enumerate([(g1_in, g1_ref), (g2_in, g2_ref)])]
    for copy in ins:
        copy.start()
    mine, total = counts(ec_ref)
    wsb, wsr = scores(ws_ref)
    gs_ref[...] = gs_in[...]
    loss_ref[...] = loss_in[...]
    gsrc_ref[...] = jnp.zeros_like(gsrc_ref)
    scale = 1.0 / (NEG * total)
    live = jnp.where(iota((EDGES, LANES), 0).astype(F32) < mine, scale, 0.0)

    def head(score, a2):
        loss_ref[...] += jnp.sum(live * softplus(score), axis=0, keepdims=True)
        ds = live * jax.nn.sigmoid(score)
        gs_ref[...] += jnp.sum(wide(ds) * a2, axis=0, keepdims=True)
        return ds

    w1 = w1_ref[...] * BF16(0.5)
    w2 = w2_ref[...] * BF16(0.5)

    first.wait()

    def step(i, carry):
        src = semb_ref[...].astype(F32)
        ks = [4 * i + j for j in range(4)]
        negs = [neg_ref[pl.ds(k, 1), :] for k in ks]
        xs = [(src * n).astype(BF16) for n in negs]

        def ready():
            @pl.when(i == 0)
            def _():
                for copy in ins:
                    copy.wait()

        def summed():
            for at, kept in enumerate([g1_ref, g2_ref]):
                @pl.when(jnp.logical_and(i == NEG // 4 - 1, core == at))
                def _():
                    pltpu.make_async_copy(kept, keep_hbm, sems.at[3]).start()

        dxs = decode_parts(xs, [head] * 4, w1, w2, wsb, wsr, g1_ref, g2_ref, ready, summed)
        gsrc = gsrc_ref[...]
        for k, n, dx in zip(ks, negs, dxs):
            gsrc = gsrc + dx * n
            gneg_ref[pl.ds(k, 1), :] = jnp.sum(dx * src, axis=0, keepdims=True)
        gsrc_ref[...] = gsrc
        return carry

    lax.fori_loop(0, NEG // 4, step, 0)
    out = pltpu.make_async_copy(gsrc_ref, gsrc_hbm, sems.at[2])
    out.start()
    loss = jnp.concatenate([loss_ref[...], jnp.zeros((1, WIDTH - LANES), F32)], axis=1)
    extra = jnp.concatenate([gneg_ref[...] * 2.0, gs_ref[...], loss, jnp.zeros((6, WIDTH), F32)], axis=0)
    extra_ref[...] = extra
    send_ref[WIDTH:, :] = extra
    for at, (kept, sent) in enumerate([(g1_ref, g2_ref), (g2_ref, g1_ref)]):
        @pl.when(core == at)
        def _():
            send_ref[0:WIDTH, :] = sent[...]
            pltpu.make_async_copy(kept, keep_hbm, sems.at[3]).wait()

    out.wait()


def negative(semb, negs, w1, w2, ws, ec, g1, g2, gs, loss):
    return pl.pallas_call(
        negative_kernel,
        in_specs=[HBM] + [VMEM] * 5 + [HBM] * 2 + [VMEM] * 2,
        out_specs=[HBM, VMEM, HBM, VMEM],
        out_shape=[
            pltpu.HBM((WIDTH, WIDTH), F32),
            jax.ShapeDtypeStruct((TALL, WIDTH), F32),
            pltpu.HBM((EDGES, WIDTH), F32),
            jax.ShapeDtypeStruct((TALL - WIDTH, WIDTH), F32),
        ],
        scratch_shapes=[pltpu.VMEM((WIDTH, WIDTH), F32)] * 3 + [
            pltpu.VMEM((1, WIDTH), F32),
            pltpu.VMEM((1, LANES), F32),
            pltpu.VMEM((NEG, WIDTH), F32),
            pltpu.VMEM((EDGES, WIDTH), BF16),
            pltpu.SemaphoreType.DMA((5,)),
        ],
        compiler_params=pltpu.CompilerParams(vmem_limit_bytes=40 * MIB),
        cost_estimate=pl.CostEstimate(flops=20_000_000_000, bytes_accessed=8 * MIB, transcendentals=0),
        name="negative",
    )(*in_hbm(semb), negs, w1, w2, ws, ec, *in_hbm(g1, g2), gs, loss)


def join_kernel(keep_hbm, got_ref, mine_ref, out_ref, keep_ref, sems):
    count = WIDTH // 4
    copies = []
    for q in range(4):
        rows = pl.ds(q * count, count)
        copies.append(pltpu.make_async_copy(keep_hbm.at[rows, :], keep_ref.at[rows, :], sems.at[q]))
        copies[q].start()
    extra = mine_ref[...] + got_ref[WIDTH:, :]
    tiles = []
    for k in range(NEG + 2):
        block = jnp.concatenate([extra[k:k + 1, LANES * j:LANES * (j + 1)] for j in range(4)], axis=0)
        high = block.astype(BF16).astype(F32)
        tiles += [high, block - high]
    tiles.append(jnp.zeros((WIDTH - 8 * (NEG + 2), LANES), F32))
    out_ref[:, WIDTH:] = stack(tiles).astype(BF16)
    for q in range(4):
        rows = pl.ds(q * count, count)
        copies[q].wait()
        out_ref[rows, 0:WIDTH] = (keep_ref[rows, :] + got_ref[rows, :]).astype(BF16)


def join(keep, got, mine):
    return pl.pallas_call(
        join_kernel,
        in_specs=[HBM, VMEM, VMEM],
        out_specs=VMEM,
        out_shape=jax.ShapeDtypeStruct((WIDTH, WIDE), BF16),
        scratch_shapes=[pltpu.VMEM((WIDTH, WIDTH), F32), pltpu.SemaphoreType.DMA((4,))],
        compiler_params=pltpu.CompilerParams(vmem_limit_bytes=16 * MIB),
        name="join",
    )(*in_hbm(keep), got, mine)


def block_of(node):
    local = node - lax.axis_index(AXES) * ROWS
    held = jnp.logical_and(local >= 0, local < ROWS)
    return held, jnp.where(held, local // 8 * 8, 0)


def scatter_kernel(gsrc_ref, back_ref, pos_ref, src_ref, gdst_ref, row_ref, neg_ref,
                   out_ref, near_ref, shi, slo, dst):
    block = out_ref.shape[0]

    @pl.when(pl.program_id(0) == 0)
    def _():
        placed = onehot_rows(column(pos_ref[...]), SLOTS)
        used = column(row_ref[0:1, :]) >= 0
        dst[...] = jnp.where(wide(used.astype(F32)) > 0.5, gdst_ref[...].astype(F32), 0.0).astype(BF16)
        shi[...], slo[...] = split(gsrc_ref[...] * 2.0 + mm(placed, back_ref[...]))
        near_ref[...] = jnp.zeros_like(near_ref)

    base = pl.program_id(0) * block
    mine = one(iota((block, EDGES), 0) + base == src_ref[...])
    theirs = one(iota((block, SLOTS), 0) + base == row_ref[0:1, :].astype(jnp.int32))
    out_ref[...] = (mm(mine, shi[...]) + mm(mine, slo[...])) + mm(theirs, dst[...])
    for k in range(NEG):
        held, at = block_of(neg_ref[k])

        @pl.when(jnp.logical_and(held, jnp.logical_and(at >= base, at < base + block)))
        def _():
            near_ref[k] = out_ref[pl.ds(pl.multiple_of(jnp.clip(at - base, 0, block - 8), 8), 8), :]


def scatter(gsrc, back, pos, src_row, gdst, rows, neg_ids):
    block = 512
    whole = lambda shape: pl.BlockSpec(shape, lambda i: (0, 0))
    return pl.pallas_call(
        scatter_kernel,
        grid=(ROWS // block,),
        in_specs=[
            whole((EDGES, WIDTH)), whole((SLOTS, WIDTH)), whole((1, EDGES)),
            whole((1, EDGES)), whole((SLOTS, WIDTH)), whole((8, SLOTS)), SMEM,
        ],
        out_specs=[pl.BlockSpec((block, WIDTH), lambda i: (i, 0)), pl.BlockSpec((NEG, 8, WIDTH), lambda i: (0, 0, 0))],
        out_shape=[jax.ShapeDtypeStruct((ROWS, WIDTH), F32), jax.ShapeDtypeStruct((NEG, 8, WIDTH), F32)],
        scratch_shapes=[
            pltpu.VMEM((EDGES, WIDTH), BF16), pltpu.VMEM((EDGES, WIDTH), BF16),
            pltpu.VMEM((SLOTS, WIDTH), BF16),
        ],
        compiler_params=pltpu.CompilerParams(vmem_limit_bytes=24 * MIB),
        cost_estimate=pl.CostEstimate(flops=7_000_000_000, bytes_accessed=10 * MIB, transcendentals=0),
        name="scatter",
    )(gsrc, back, pos, src_row, gdst, rows, neg_ids)


def total_kernel(parts_ref, out_ref):
    def step(i, acc):
        rows = pl.ds(pl.multiple_of(i * 64, 64), 64)
        part = parts_ref[rows, :].astype(F32)
        for j in range(8):
            acc = acc + part[8 * j:8 * j + 8, :]
        return acc

    acc = lax.fori_loop(0, GROUP // 8, step, jnp.zeros((CAP, WIDE), F32))
    extra = acc[:, WIDTH:]
    extra = extra[0:4, :] + extra[4:8, :]
    high = extra.astype(BF16).astype(F32)
    line = jnp.concatenate([acc[:, :WIDTH], jnp.concatenate([high, extra - high], axis=0)], axis=1)
    both = jnp.concatenate([line, line], axis=0).astype(BF16)

    def store(i, carry):
        out_ref[pl.ds(pl.multiple_of(i * 16, 16), 16), :] = both
        return carry

    lax.fori_loop(0, GROUP // 2, store, 0)


def total_up(parts):
    return pl.pallas_call(
        total_kernel,
        in_specs=[VMEM],
        out_specs=VMEM,
        out_shape=jax.ShapeDtypeStruct((WIDTH, WIDE), BF16),
        compiler_params=pltpu.CompilerParams(vmem_limit_bytes=16 * MIB),
        name="total_up",
    )(parts)


def sent_out(sums_ref, f_ref, out_hbm, sems):
    copies = []
    for h in range(4):
        rows = pl.ds(h * 128, 128)
        f_ref[rows, :] = sums_ref[rows, 0:WIDTH].astype(F32)
        copies.append(pltpu.make_async_copy(f_ref.at[rows, :], out_hbm.at[rows, :], sems.at[h]))
        copies[h].start()
    return copies


def own_kernel(sums_ref, neg_ref, near_ref, grads_in, g1_hbm, g2_hbm, gs_ref, loss_ref, grads_ref, half_ref, blocks, sems, out_sems):
    mine, bases = zip(*[block_of(neg_ref[k]) for k in range(NEG)])
    me = lax.axis_index(AXES)

    def put(k):
        rows = pl.ds(pl.multiple_of(bases[k], 8), 8)
        return pltpu.make_async_copy(blocks.at[k], grads_ref.at[rows, :], sems.at[k])

    extra = sums_ref[0:8 * (NEG + 2), WIDTH:].astype(F32)

    def line(k):
        block = extra[8 * k:8 * k + 4, :] + extra[8 * k + 4:8 * k + 8, :]
        return jnp.concatenate([block[j:j + 1, :] for j in range(4)], axis=1)

    gs_ref[...] = line(NEG)
    loss_ref[...] = line(NEG + 1)[:, 0:LANES]
    sub = iota((8, WIDTH), 0)
    for k in range(NEG):
        block = near_ref[k]
        for j in range(NEG):
            local = neg_ref[j] - me * ROWS
            hit = jnp.logical_and(mine[j], bases[j] == bases[k])
            at = jnp.where(hit, local - bases[k], -1)
            block = block + jnp.where(sub == at, line(j), 0.0)
        blocks[k] = block

        @pl.when(mine[k])
        def _():
            put(k).start()

    core = lax.axis_index("c")
    for at, g_hbm in enumerate([g1_hbm, g2_hbm]):
        @pl.when(core == at)
        def _():
            sent_out(sums_ref, half_ref, g_hbm, out_sems.at[at])

    for k in range(NEG):
        @pl.when(mine[k])
        def _():
            put(k).wait()

    for at, g_hbm in enumerate([g1_hbm, g2_hbm]):
        @pl.when(core == at)
        def _():
            for h in range(4):
                rows = pl.ds(h * 128, 128)
                pltpu.make_async_copy(half_ref.at[rows, :], g_hbm.at[rows, :], out_sems.at[at, h]).wait()


def finish_own(sums, neg_ids, near, grads):
    return pl.pallas_call(
        own_kernel,
        in_specs=[VMEM, SMEM, VMEM, pl.BlockSpec(memory_space=pl.ANY)],
        out_specs=[HBM, HBM, VMEM, VMEM, pl.BlockSpec(memory_space=pl.ANY)],
        out_shape=[
            pltpu.HBM((WIDTH, WIDTH), F32),
            pltpu.HBM((WIDTH, WIDTH), F32),
            jax.ShapeDtypeStruct((1, WIDTH), F32),
            jax.ShapeDtypeStruct((1, LANES), F32),
            jax.ShapeDtypeStruct((ROWS, WIDTH), F32),
        ],
        input_output_aliases={3: 4},
        scratch_shapes=[
            pltpu.VMEM((WIDTH, WIDTH), F32),
            pltpu.VMEM((NEG, 8, WIDTH), F32),
            pltpu.SemaphoreType.DMA((NEG,)),
            pltpu.SemaphoreType.DMA((2, 4)),
        ],
        compiler_params=pltpu.CompilerParams(vmem_limit_bytes=16 * MIB),
        cost_estimate=pl.CostEstimate(flops=1_000_000, bytes_accessed=2 * MIB, transcendentals=0),
        name="finish_own",
    )(sums, neg_ids, near, grads)


def other_kernel(other_ref, g1_in, g2_in, g1_hbm, g2_hbm, rest_ref, sems):
    core = lax.axis_index("c")
    for at, g_hbm in enumerate([g2_hbm, g1_hbm]):
        @pl.when(core == at)
        def _():
            for copy in sent_out(other_ref, rest_ref, g_hbm, sems.at[at]):
                copy.wait()


def finish_other(other, g1, g2):
    return pl.pallas_call(
        other_kernel,
        in_specs=[VMEM, HBM, HBM],
        out_specs=[HBM, HBM],
        out_shape=[pltpu.HBM((WIDTH, WIDTH), F32)] * 2,
        input_output_aliases={1: 0, 2: 1},
        scratch_shapes=[pltpu.VMEM((WIDTH, WIDTH), F32), pltpu.SemaphoreType.DMA((2, 4))],
        compiler_params=pltpu.CompilerParams(vmem_limit_bytes=16 * MIB),
        name="finish_other",
    )(other, *in_hbm(g1, g2))


def exchange(rows, axes):
    parts = rows.reshape(-1, CAP, rows.shape[1])
    out = lax.all_to_all(parts, axes, split_axis=0, concat_axis=0, tiled=True)
    return out.reshape(rows.shape)


def swap(rows):
    return lax.ppermute(rows, "c", [(0, 1), (1, 0)])


def flip(rows, by):
    return lax.ppermute(rows, "x", [(i, i ^ by) for i in range(4)])


def body(embeddings, w_first, w_second, w_score, src_row, dst_owner, dst_row, edge_count, neg_ids):
    ec = edge_count.reshape(1, DEVICES)
    ws = w_score.reshape(1, WIDTH)
    src_row = src_row.reshape(1, EDGES)
    push, semb, pos = prepare(
        embeddings, src_row, dst_owner.reshape(1, EDGES), dst_row.reshape(1, EDGES), ec, neg_ids
    )
    recv = exchange(push, AXES)
    negs = pick(recv)
    negs = negs + swap(negs)
    near_x = flip(negs, 1)
    ret, gdst, rows, g1, g2, gs, loss = positive(recv, embeddings, w_first, w_second, ws, ec)
    ret, near_x = lax.optimization_barrier((ret, near_x))
    negs = negs + near_x
    negs = negs + flip(negs, 2)
    back = exchange(ret, AXES)
    keep, send, gsrc, extra = negative(semb, negs, w_first, w_second, ws, ec, g1, g2, gs, loss)
    send, back = lax.optimization_barrier((send, back))
    payload = join(keep, swap(send), extra)
    parts = exchange(payload, CHIPS)
    grads, near = scatter(gsrc, back, pos, src_row, gdst, rows, neg_ids)
    parts, grads = lax.optimization_barrier((parts, grads))
    sums = exchange(total_up(parts), CHIPS)
    other = swap(sums)
    g1, g2, gs, loss, grads = finish_own(sums, neg_ids, near, grads)
    g1, g2 = finish_other(other, g1, g2)
    return grads, g1, g2, gs.reshape(WIDTH), loss[0, 0]


def solution(mesh):
    mesh = Mesh(mesh.devices.reshape(4, 4, 2, 4), AXES)
    in_specs = (
        P(AXES, None), P(), P(), P(), P(AXES), P(AXES, None), P(AXES), P(), P(),
    )
    out_specs = (P(AXES, None), P(), P(), P(), P())
    return jax.shard_map(body, mesh=mesh, in_specs=in_specs, out_specs=out_specs, check_vma=False)
```

```python
import jax
import jax.numpy as jnp
from jax import lax
from jax.experimental import pallas as pl
from jax.experimental.pallas import tpu as pltpu
from jax.sharding import Mesh, PartitionSpec as P

F32 = jnp.float32
BF16 = jnp.bfloat16
AXES = ("z", "y", "c", "x")
CHIPS = ("z", "y", "x")
VMEM = pl.BlockSpec(memory_space=pltpu.VMEM)
SMEM = pl.BlockSpec(memory_space=pltpu.SMEM)
HBM = pl.BlockSpec(memory_space=pltpu.HBM)
MIB = 1 << 20


def in_hbm(*arrays):
    return tuple(pltpu.with_memory_space_constraint(a, pltpu.HBM) for a in arrays)


DEVICES = 128
GROUP = 64
ROWS = 2048
EDGES = 512
WIDTH = 512
NEG = 8
CAP = 8
SLOTS = DEVICES * CAP
LANES = 128
WIDE = WIDTH + LANES
TALL = WIDTH + 16


def mm(a, b):
    return jnp.dot(a, b, preferred_element_type=F32)


def mm_nt(a, b):
    return lax.dot_general(a, b, (((1,), (1,)), ((), ())), preferred_element_type=F32)


def mm_tn(a, b):
    return lax.dot_general(a, b, (((0,), (0,)), ((), ())), preferred_element_type=F32)


def wide(value):
    return jnp.concatenate([value] * (WIDTH // LANES), axis=1)


def iota(shape, dim):
    return lax.broadcasted_iota(jnp.int32, shape, dim)


def one(mask):
    return jnp.where(mask, 1.0, 0.0).astype(BF16)


def column(row):
    return jnp.transpose(jnp.broadcast_to(row.astype(F32), (LANES, row.shape[1]))).astype(jnp.int32)


def onehot_rows(col, count):
    lane = iota(col.shape, 1)
    return jnp.concatenate([one(col == lane + LANES * j) for j in range(count // LANES)], axis=1)


def split(value):
    high = value.astype(BF16)
    return high, (value - high.astype(F32)).astype(BF16)


def softplus(value):
    return jnp.maximum(value, 0.0) + jnp.log1p(jnp.exp(-jnp.abs(value)))


def gate(half):
    t = jnp.tanh(half)
    m = half * t
    return half + m, (1.0 + t) * (1.0 + (half - m))


def counts(ec_ref):
    me = lax.axis_index(AXES)
    ec = ec_ref[...]
    mine = jnp.sum(jnp.where(iota(ec.shape, 1) == me, ec, 0).astype(F32), axis=1, keepdims=True)
    return mine, jnp.sum(ec.astype(F32), axis=1, keepdims=True)


def prepare_kernel(emb_hbm, src_hbm, owner_hbm, dst_hbm, ec_hbm, neg_hbm, push_ref, semb_hbm, pos_ref,
                   emb_ref, src_ref, owner_ref, dst_ref, ec_ref, neg_ref, semb_ref, sems):
    pairs = [(neg_hbm, neg_ref), (ec_hbm, ec_ref), (owner_hbm, owner_ref), (src_hbm, src_ref),
             (dst_hbm, dst_ref), (emb_hbm, emb_ref)]
    copies = [pltpu.make_async_copy(a, b, sems.at[i]) for i, (a, b) in enumerate(pairs)]
    for copy in copies:
        copy.start()
    for copy in copies[:-1]:
        copy.wait()
    me = lax.axis_index(AXES)
    mine, _ = counts(ec_ref)
    live = iota((1, EDGES), 1).astype(F32) < mine
    owner = jnp.where(live, owner_ref[...], -1)
    named = one(iota((DEVICES, EDGES), 0) == owner)
    before = one(iota((EDGES, EDGES), 0) < iota((EDGES, EDGES), 1))
    rank = jnp.sum(mm(named, before) * named.astype(F32), axis=0, keepdims=True)
    pos = jnp.where(live, owner * CAP + rank.astype(jnp.int32), -1)
    pos_ref[...] = pos
    row = column(dst_ref[...])
    lane = iota((EDGES, LANES), 1)
    meta = jnp.where(lane == 0, row // 64, jnp.where(lane == 1, row % 64, jnp.where(lane == 2, 1, 0)))
    meta = meta.astype(F32).astype(BF16)
    sub = iota((2 * NEG, LANES), 0)
    local = jnp.full((2 * NEG, LANES), -1, jnp.int32)
    for k in range(NEG):
        local = jnp.where(sub == k, neg_ref[k] - me * ROWS, local)
    chosen = onehot_rows(jnp.concatenate([column(src_ref[...]), local], axis=0), ROWS)
    copies[-1].wait()
    emb = emb_ref[...]
    found = mm(chosen, emb)
    semb = found[0:EDGES, :].astype(BF16)
    semb_ref[...] = semb
    out = pltpu.make_async_copy(semb_ref, semb_hbm, sems.at[6])
    out.start()
    offers = found[EDGES:EDGES + NEG, :]
    high = iota((NEG, LANES), 1) >= LANES // 2
    pieces = []
    for q in range(4):
        tile = offers[:, LANES * q:LANES * (q + 1)]
        pieces += [jnp.where(high, pltpu.roll(tile, LANES // 2, 1), 0.0), jnp.where(high, tile, 0.0)]
    pieces = jnp.concatenate(pieces, axis=0)
    count = SLOTS // 4
    for q in range(4):
        rows = pl.ds(q * count, count)
        place = one(iota((count, EDGES), 0) + q * count == pos)
        push_ref[rows, 0:WIDTH] = mm(place, semb).astype(BF16)
        push_ref[rows, WIDTH:] = (mm(place, meta) + jnp.concatenate([pieces] * (count // 64), axis=0)).astype(BF16)
    out.wait()


def prepare(emb, src_row, owner, dst_row, ec, neg_ids):
    return pl.pallas_call(
        prepare_kernel,
        in_specs=[HBM] * 6,
        out_specs=[VMEM, HBM, VMEM],
        out_shape=[
            pltpu.VMEM((SLOTS, WIDE), BF16),
            pltpu.HBM((EDGES, WIDTH), BF16),
            jax.ShapeDtypeStruct((1, EDGES), jnp.int32),
        ],
        scratch_shapes=[
            pltpu.VMEM((ROWS, WIDTH), BF16),
            pltpu.VMEM((1, EDGES), jnp.int32),
            pltpu.VMEM((1, EDGES), jnp.int32),
            pltpu.VMEM((1, EDGES), jnp.int32),
            pltpu.VMEM((1, DEVICES), jnp.int32),
            pltpu.SMEM((NEG,), jnp.int32),
            pltpu.VMEM((EDGES, WIDTH), BF16),
            pltpu.SemaphoreType.DMA((7,)),
        ],
        compiler_params=pltpu.CompilerParams(vmem_limit_bytes=24 * MIB),
        name="prepare",
    )(*in_hbm(emb, src_row, owner, dst_row, ec, neg_ids))


def pick_kernel(recv_ref, out_ref):
    told = recv_ref[:, WIDTH:].astype(F32)
    piece = jnp.sum(told.reshape(DEVICES, CAP, LANES), axis=0)
    part = lax.axis_index("c") * 4 + lax.axis_index("x")
    high = iota((NEG, LANES), 1) >= LANES // 2
    for i in range(4):
        low = jnp.logical_and(jnp.logical_not(high), part == 2 * i)
        tile = jnp.where(low, pltpu.roll(piece, LANES // 2, 1), 0.0)
        tile = jnp.where(jnp.logical_and(high, part == 2 * i + 1), piece, tile)
        out_ref[:, LANES * i:LANES * (i + 1)] = tile


def pick(recv):
    return pl.pallas_call(
        pick_kernel,
        in_specs=[VMEM],
        out_specs=VMEM,
        out_shape=jax.ShapeDtypeStruct((NEG, WIDTH), F32),
        compiler_params=pltpu.CompilerParams(vmem_limit_bytes=16 * MIB),
        name="pick",
    )(recv)


def stack(parts):
    return jnp.concatenate(parts, axis=0) if len(parts) > 1 else parts[0]


def decode_parts(xs, heads, w1, w2, wsb, wsr, g1_ref, g2_ref, ready=None, summed=None):
    first = [gate(mm(x, w1)) for x in xs]
    a1s = [a.astype(BF16) for a, _ in first]
    second = [gate(mm(a, w2)) for a in a1s]
    dz2s = []
    for (a2, slope), head in zip(second, heads):
        ds = wide(head(mm(a2.astype(BF16), wsb), a2))
        dz2s.append((ds * (wsr * slope)).astype(BF16))
    dz1s = [(mm_nt(dz2, w2) * slope).astype(BF16) for dz2, (_, slope) in zip(dz2s, first)]
    if ready is not None:
        ready()
    g2_ref[...] += mm_tn(stack(a1s), stack(dz2s))
    g1_ref[...] += mm_tn(stack(xs), stack(dz1s))
    if summed is not None:
        summed()
    return [mm_nt(dz1, w1) for dz1 in dz1s]


def scores(ws_ref):
    ws = ws_ref[...].astype(F32)
    return jnp.transpose(jnp.broadcast_to(ws, (LANES, WIDTH))).astype(BF16), ws * 0.5


def positive_kernel(recv_ref, emb_ref, w1_hbm, w2_hbm, ws_ref, ec_ref,
                    ret_ref, gdst_hbm, row_ref, g1_hbm, g2_hbm, gs_ref, loss_ref,
                    w1_ref, w2_ref, gdst_ref, g1_ref, g2_ref, sems, out_sems):
    ins = [pltpu.make_async_copy(a, b, sems.at[i]) for i, (a, b) in enumerate([(w1_hbm, w1_ref), (w2_hbm, w2_ref)])]
    for copy in ins:
        copy.start()
    _, total = counts(ec_ref)
    wsb, wsr = scores(ws_ref)
    g1_ref[...] = jnp.zeros_like(g1_ref)
    g2_ref[...] = jnp.zeros_like(g2_ref)
    gs_ref[...] = jnp.zeros_like(gs_ref)
    loss_ref[...] = jnp.zeros_like(loss_ref)
    spread = iota((LANES, 2 * LANES), 0)
    right = iota((LANES, 2 * LANES), 1) >= LANES
    table = jnp.where(
        right,
        jnp.where(spread == 2, 1.0, 0.0),
        jnp.where(spread == 0, 64.0, jnp.where(spread == 1, 1.0, 0.0)),
    ).astype(BF16)
    lane = iota((8, LANES), 1)
    sub = iota((8, LANES), 0)
    flag = jnp.where(jnp.logical_and(sub == 0, lane == 2), 1.0, 0.0).astype(BF16)
    taken = mm_nt(flag, recv_ref[:, WIDTH:WIDE])[0:1, :]
    taken = jnp.concatenate([taken[:, LANES * j:LANES * (j + 1)] for j in range(8)], axis=0)
    before = one(iota((LANES, LANES), 0) < iota((LANES, LANES), 1))
    place = mm(taken.astype(BF16), before)
    held = jnp.broadcast_to(jnp.sum(taken, axis=1, keepdims=True), (8, LANES))
    offset = jnp.zeros((8, LANES), F32)
    for j in range(7):
        offset = offset + jnp.where(sub > j, held[j:j + 1, :], 0.0)
    place = jnp.where(taken > 0.5, place + offset, -1.0).astype(jnp.int32)
    place = jnp.concatenate([place[j:j + 1, :] for j in range(8)], axis=1)
    place_col = column(place)
    half = SLOTS // 2
    rounds = jnp.where(jnp.sum(taken) > half, 2, 1)
    row_ref[...] = jnp.full(row_ref.shape, -1.0, F32)

    def step(h, carry):
        rows = pl.ds(pl.multiple_of(h * half, half), half)
        chosen = one(iota((half, SLOTS), 0) + h * half == place)
        got = mm(chosen, recv_ref[...])
        src = got[:, 0:WIDTH]
        told = mm(got[:, WIDTH:].astype(BF16), table)
        live = told[:, LANES:]
        row = jnp.where(live > 0.5, told[:, :LANES], -1.0)
        row_ref[:, rows] = jnp.transpose(row)[0:8, :]
        dst = mm(onehot_rows(row.astype(jnp.int32), ROWS), emb_ref[...])

        def head(score, a2):
            loss_ref[...] += jnp.sum(live * softplus(-score), axis=0, keepdims=True) / total
            ds = -live * jax.nn.sigmoid(-score) / total
            gs_ref[...] += jnp.sum(wide(ds) * a2, axis=0, keepdims=True)
            return ds

        outs = [
            pltpu.make_async_copy(g1_ref, g1_hbm, out_sems.at[0]),
            pltpu.make_async_copy(g2_ref, g2_hbm, out_sems.at[1]),
            pltpu.make_async_copy(gdst_ref.at[rows, :], gdst_hbm.at[rows, :], out_sems.at[2]),
        ]

        def summed():
            for copy in outs[:2]:
                copy.start()

        @pl.when(h == 0)
        def _():
            for copy in ins:
                copy.wait()

        w1 = w1_ref[...] * BF16(0.5)
        w2 = w2_ref[...] * BF16(0.5)

        (dx,) = decode_parts([(src * dst).astype(BF16)], [head], w1, w2, wsb, wsr, g1_ref, g2_ref, None, summed)
        dx = dx * 2.0
        gdst_ref[rows, :] = (dx * src).astype(BF16)
        outs[2].start()
        back = mm(onehot_rows(place_col - h * half, half), (dx * dst).astype(BF16))

        @pl.when(h == 0)
        def _():
            ret_ref[...] = back.astype(BF16)

        @pl.when(h > 0)
        def _():
            ret_ref[...] = (ret_ref[...].astype(F32) + back).astype(BF16)

        for copy in outs:
            copy.wait()
        return carry

    lax.fori_loop(0, rounds, step, 0)


def positive(recv, emb, w1, w2, ws, ec):
    return pl.pallas_call(
        positive_kernel,
        in_specs=[VMEM, VMEM, HBM, HBM, VMEM, VMEM],
        out_specs=[VMEM, HBM, VMEM, HBM, HBM, VMEM, VMEM],
        out_shape=[
            pltpu.VMEM((SLOTS, WIDTH), BF16),
            pltpu.HBM((SLOTS, WIDTH), BF16),
            jax.ShapeDtypeStruct((8, SLOTS), F32),
            pltpu.HBM((WIDTH, WIDTH), F32),
            pltpu.HBM((WIDTH, WIDTH), F32),
            jax.ShapeDtypeStruct((1, WIDTH), F32),
            jax.ShapeDtypeStruct((1, LANES), F32),
        ],
        scratch_shapes=[
            pltpu.VMEM((WIDTH, WIDTH), BF16),
            pltpu.VMEM((WIDTH, WIDTH), BF16),
            pltpu.VMEM((SLOTS, WIDTH), BF16),
            pltpu.VMEM((WIDTH, WIDTH), F32),
            pltpu.VMEM((WIDTH, WIDTH), F32),
            pltpu.SemaphoreType.DMA((2,)),
            pltpu.SemaphoreType.DMA((3,)),
        ],
        compiler_params=pltpu.CompilerParams(vmem_limit_bytes=36 * MIB),
        cost_estimate=pl.CostEstimate(flops=6_000_000_000, bytes_accessed=12 * MIB, transcendentals=0),
        name="positive",
    )(recv, emb, *in_hbm(w1, w2), ws, ec)


def negative_kernel(semb_hbm, neg_ref, w1_ref, w2_ref, ws_ref, ec_ref, g1_in, g2_in, gs_in, loss_in,
                    keep_hbm, send_ref, gsrc_hbm, extra_ref, gsrc_ref, g1_ref, g2_ref, gs_ref, loss_ref, gneg_ref,
                    semb_ref, sems, out_sems):
    core = lax.axis_index("c")
    first = pltpu.make_async_copy(semb_hbm, semb_ref, sems.at[4])
    first.start()
    ins = [pltpu.make_async_copy(a, b, sems.at[i]) for i, (a, b) in enumerate([(g1_in, g1_ref), (g2_in, g2_ref)])]
    for copy in ins:
        copy.start()
    mine, total = counts(ec_ref)
    wsb, wsr = scores(ws_ref)
    gs_ref[...] = gs_in[...]
    loss_ref[...] = loss_in[...]
    gsrc_ref[...] = jnp.zeros_like(gsrc_ref)
    scale = 1.0 / (NEG * total)
    live = jnp.where(iota((EDGES, LANES), 0).astype(F32) < mine, scale, 0.0)

    def head(score, a2):
        loss_ref[...] += jnp.sum(live * softplus(score), axis=0, keepdims=True)
        ds = live * jax.nn.sigmoid(score)
        gs_ref[...] += jnp.sum(wide(ds) * a2, axis=0, keepdims=True)
        return ds

    w1 = w1_ref[...] * BF16(0.5)
    w2 = w2_ref[...] * BF16(0.5)

    first.wait()

    def step(i, carry):
        src = semb_ref[...].astype(F32)
        ks = [4 * i + j for j in range(4)]
        negs = [neg_ref[pl.ds(k, 1), :] for k in ks]
        xs = [(src * n).astype(BF16) for n in negs]

        def ready():
            @pl.when(i == 0)
            def _():
                for copy in ins:
                    copy.wait()

        def summed():
            for at, kept in enumerate([g1_ref, g2_ref]):
                @pl.when(jnp.logical_and(i == NEG // 4 - 1, core == at))
                def _():
                    pltpu.make_async_copy(kept, keep_hbm, sems.at[3]).start()

        dxs = decode_parts(xs, [head] * 4, w1, w2, wsb, wsr, g1_ref, g2_ref, ready, summed)
        for q in range(4):
            rows = slice(q * 128, q * 128 + 128)
            gsrc = gsrc_ref[rows, :]
            for n, dx in zip(negs, dxs):
                gsrc = gsrc + dx[rows, :] * n
            gsrc_ref[rows, :] = gsrc

            @pl.when(i == NEG // 4 - 1)
            def _():
                outs[q].start()

        for k, dx in zip(ks, dxs):
            gneg_ref[pl.ds(k, 1), :] = jnp.sum(dx * src, axis=0, keepdims=True)
        return carry

    outs = []
    for q in range(4):
        rows = pl.ds(q * 128, 128)
        outs.append(pltpu.make_async_copy(gsrc_ref.at[rows, :], gsrc_hbm.at[rows, :], out_sems.at[q]))
    lax.fori_loop(0, NEG // 4, step, 0)
    loss = jnp.concatenate([loss_ref[...], jnp.zeros((1, WIDTH - LANES), F32)], axis=1)
    extra = jnp.concatenate([gneg_ref[...] * 2.0, gs_ref[...], loss, jnp.zeros((6, WIDTH), F32)], axis=0)
    extra_ref[...] = extra
    send_ref[WIDTH:, :] = extra
    for at, (kept, sent) in enumerate([(g1_ref, g2_ref), (g2_ref, g1_ref)]):
        @pl.when(core == at)
        def _():
            send_ref[0:WIDTH, :] = sent[...]
            pltpu.make_async_copy(kept, keep_hbm, sems.at[3]).wait()

    for out in outs:
        out.wait()


def negative(semb, negs, w1, w2, ws, ec, g1, g2, gs, loss):
    return pl.pallas_call(
        negative_kernel,
        in_specs=[HBM] + [VMEM] * 5 + [HBM] * 2 + [VMEM] * 2,
        out_specs=[HBM, VMEM, HBM, VMEM],
        out_shape=[
            pltpu.HBM((WIDTH, WIDTH), F32),
            jax.ShapeDtypeStruct((TALL, WIDTH), F32),
            pltpu.HBM((EDGES, WIDTH), F32),
            jax.ShapeDtypeStruct((TALL - WIDTH, WIDTH), F32),
        ],
        scratch_shapes=[pltpu.VMEM((WIDTH, WIDTH), F32)] * 3 + [
            pltpu.VMEM((1, WIDTH), F32),
            pltpu.VMEM((1, LANES), F32),
            pltpu.VMEM((NEG, WIDTH), F32),
            pltpu.VMEM((EDGES, WIDTH), BF16),
            pltpu.SemaphoreType.DMA((5,)),
            pltpu.SemaphoreType.DMA((4,)),
        ],
        compiler_params=pltpu.CompilerParams(vmem_limit_bytes=40 * MIB),
        cost_estimate=pl.CostEstimate(flops=20_000_000_000, bytes_accessed=8 * MIB, transcendentals=0),
        name="negative",
    )(*in_hbm(semb), negs, w1, w2, ws, ec, *in_hbm(g1, g2), gs, loss)


def join_kernel(keep_hbm, got_ref, mine_ref, out_ref, keep_ref, sems):
    count = WIDTH // 4
    copies = []
    for q in range(4):
        rows = pl.ds(q * count, count)
        copies.append(pltpu.make_async_copy(keep_hbm.at[rows, :], keep_ref.at[rows, :], sems.at[q]))
        copies[q].start()
    extra = mine_ref[...] + got_ref[WIDTH:, :]
    tiles = []
    for k in range(NEG + 2):
        block = jnp.concatenate([extra[k:k + 1, LANES * j:LANES * (j + 1)] for j in range(4)], axis=0)
        high = block.astype(BF16).astype(F32)
        tiles += [high, block - high]
    tiles.append(jnp.zeros((WIDTH - 8 * (NEG + 2), LANES), F32))
    out_ref[:, WIDTH:] = stack(tiles).astype(BF16)
    for q in range(4):
        rows = pl.ds(q * count, count)
        copies[q].wait()
        out_ref[rows, 0:WIDTH] = (keep_ref[rows, :] + got_ref[rows, :]).astype(BF16)


def join(keep, got, mine):
    return pl.pallas_call(
        join_kernel,
        in_specs=[HBM, VMEM, VMEM],
        out_specs=VMEM,
        out_shape=jax.ShapeDtypeStruct((WIDTH, WIDE), BF16),
        scratch_shapes=[pltpu.VMEM((WIDTH, WIDTH), F32), pltpu.SemaphoreType.DMA((4,))],
        compiler_params=pltpu.CompilerParams(vmem_limit_bytes=16 * MIB),
        name="join",
    )(*in_hbm(keep), got, mine)


def block_of(node):
    local = node - lax.axis_index(AXES) * ROWS
    held = jnp.logical_and(local >= 0, local < ROWS)
    return held, jnp.where(held, local // 8 * 8, 0)


def scatter_kernel(gsrc_ref, back_ref, pos_ref, src_ref, gdst_ref, row_ref, neg_ref,
                   out_ref, near_ref, shi, slo, dst):
    block = out_ref.shape[0]

    @pl.when(pl.program_id(0) == 0)
    def _():
        placed = onehot_rows(column(pos_ref[...]), SLOTS)
        used = column(row_ref[0:1, :]) >= 0
        dst[...] = jnp.where(wide(used.astype(F32)) > 0.5, gdst_ref[...].astype(F32), 0.0).astype(BF16)
        shi[...], slo[...] = split(gsrc_ref[...] * 2.0 + mm(placed, back_ref[...]))
        near_ref[...] = jnp.zeros_like(near_ref)

    base = pl.program_id(0) * block
    mine = one(iota((block, EDGES), 0) + base == src_ref[...])
    theirs = one(iota((block, SLOTS), 0) + base == row_ref[0:1, :].astype(jnp.int32))
    out_ref[...] = (mm(mine, shi[...]) + mm(mine, slo[...])) + mm(theirs, dst[...])
    for k in range(NEG):
        held, at = block_of(neg_ref[k])

        @pl.when(jnp.logical_and(held, jnp.logical_and(at >= base, at < base + block)))
        def _():
            near_ref[k] = out_ref[pl.ds(pl.multiple_of(jnp.clip(at - base, 0, block - 8), 8), 8), :]


def scatter(gsrc, back, pos, src_row, gdst, rows, neg_ids):
    block = 512
    whole = lambda shape: pl.BlockSpec(shape, lambda i: (0, 0))
    return pl.pallas_call(
        scatter_kernel,
        grid=(ROWS // block,),
        in_specs=[
            whole((EDGES, WIDTH)), whole((SLOTS, WIDTH)), whole((1, EDGES)),
            whole((1, EDGES)), whole((SLOTS, WIDTH)), whole((8, SLOTS)), SMEM,
        ],
        out_specs=[pl.BlockSpec((block, WIDTH), lambda i: (i, 0)), pl.BlockSpec((NEG, 8, WIDTH), lambda i: (0, 0, 0))],
        out_shape=[jax.ShapeDtypeStruct((ROWS, WIDTH), F32), jax.ShapeDtypeStruct((NEG, 8, WIDTH), F32)],
        scratch_shapes=[
            pltpu.VMEM((EDGES, WIDTH), BF16), pltpu.VMEM((EDGES, WIDTH), BF16),
            pltpu.VMEM((SLOTS, WIDTH), BF16),
        ],
        compiler_params=pltpu.CompilerParams(vmem_limit_bytes=24 * MIB),
        cost_estimate=pl.CostEstimate(flops=7_000_000_000, bytes_accessed=10 * MIB, transcendentals=0),
        name="scatter",
    )(gsrc, back, pos, src_row, gdst, rows, neg_ids)


def total_kernel(parts_ref, out_ref):
    def step(i, acc):
        rows = pl.ds(pl.multiple_of(i * 64, 64), 64)
        part = parts_ref[rows, :].astype(F32)
        for j in range(8):
            acc = acc + part[8 * j:8 * j + 8, :]
        return acc

    acc = lax.fori_loop(0, GROUP // 8, step, jnp.zeros((CAP, WIDE), F32))
    extra = acc[:, WIDTH:]
    extra = extra[0:4, :] + extra[4:8, :]
    high = extra.astype(BF16).astype(F32)
    line = jnp.concatenate([acc[:, :WIDTH], jnp.concatenate([high, extra - high], axis=0)], axis=1)
    both = jnp.concatenate([line, line], axis=0).astype(BF16)

    def store(i, carry):
        out_ref[pl.ds(pl.multiple_of(i * 16, 16), 16), :] = both
        return carry

    lax.fori_loop(0, GROUP // 2, store, 0)


def total_up(parts):
    return pl.pallas_call(
        total_kernel,
        in_specs=[VMEM],
        out_specs=VMEM,
        out_shape=jax.ShapeDtypeStruct((WIDTH, WIDE), BF16),
        compiler_params=pltpu.CompilerParams(vmem_limit_bytes=16 * MIB),
        name="total_up",
    )(parts)


def sent_out(sums_ref, f_ref, out_hbm, sems):
    copies = []
    for h in range(4):
        rows = pl.ds(h * 128, 128)
        f_ref[rows, :] = sums_ref[rows, 0:WIDTH].astype(F32)
        copies.append(pltpu.make_async_copy(f_ref.at[rows, :], out_hbm.at[rows, :], sems.at[h]))
        copies[h].start()
    return copies


def own_kernel(sums_ref, neg_ref, near_ref, grads_in, g1_hbm, g2_hbm, gs_ref, loss_ref, grads_ref, half_ref, blocks, sems, out_sems):
    mine, bases = zip(*[block_of(neg_ref[k]) for k in range(NEG)])
    me = lax.axis_index(AXES)

    def put(k):
        rows = pl.ds(pl.multiple_of(bases[k], 8), 8)
        return pltpu.make_async_copy(blocks.at[k], grads_ref.at[rows, :], sems.at[k])

    extra = sums_ref[0:8 * (NEG + 2), WIDTH:].astype(F32)

    def line(k):
        block = extra[8 * k:8 * k + 4, :] + extra[8 * k + 4:8 * k + 8, :]
        return jnp.concatenate([block[j:j + 1, :] for j in range(4)], axis=1)

    gs_ref[...] = line(NEG)
    loss_ref[...] = line(NEG + 1)[:, 0:LANES]
    sub = iota((8, WIDTH), 0)
    for k in range(NEG):
        block = near_ref[k]
        for j in range(NEG):
            local = neg_ref[j] - me * ROWS
            hit = jnp.logical_and(mine[j], bases[j] == bases[k])
            at = jnp.where(hit, local - bases[k], -1)
            block = block + jnp.where(sub == at, line(j), 0.0)
        blocks[k] = block

        @pl.when(mine[k])
        def _():
            put(k).start()

    core = lax.axis_index("c")
    for at, g_hbm in enumerate([g1_hbm, g2_hbm]):
        @pl.when(core == at)
        def _():
            sent_out(sums_ref, half_ref, g_hbm, out_sems.at[at])

    for k in range(NEG):
        @pl.when(mine[k])
        def _():
            put(k).wait()

    for at, g_hbm in enumerate([g1_hbm, g2_hbm]):
        @pl.when(core == at)
        def _():
            for h in range(4):
                rows = pl.ds(h * 128, 128)
                pltpu.make_async_copy(half_ref.at[rows, :], g_hbm.at[rows, :], out_sems.at[at, h]).wait()


def finish_own(sums, neg_ids, near, grads):
    return pl.pallas_call(
        own_kernel,
        in_specs=[VMEM, SMEM, VMEM, pl.BlockSpec(memory_space=pl.ANY)],
        out_specs=[HBM, HBM, VMEM, VMEM, pl.BlockSpec(memory_space=pl.ANY)],
        out_shape=[
            pltpu.HBM((WIDTH, WIDTH), F32),
            pltpu.HBM((WIDTH, WIDTH), F32),
            jax.ShapeDtypeStruct((1, WIDTH), F32),
            jax.ShapeDtypeStruct((1, LANES), F32),
            jax.ShapeDtypeStruct((ROWS, WIDTH), F32),
        ],
        input_output_aliases={3: 4},
        scratch_shapes=[
            pltpu.VMEM((WIDTH, WIDTH), F32),
            pltpu.VMEM((NEG, 8, WIDTH), F32),
            pltpu.SemaphoreType.DMA((NEG,)),
            pltpu.SemaphoreType.DMA((2, 4)),
        ],
        compiler_params=pltpu.CompilerParams(vmem_limit_bytes=16 * MIB),
        cost_estimate=pl.CostEstimate(flops=1_000_000, bytes_accessed=2 * MIB, transcendentals=0),
        name="finish_own",
    )(sums, neg_ids, near, grads)


def other_kernel(other_ref, g1_in, g2_in, g1_hbm, g2_hbm, rest_ref, sems):
    core = lax.axis_index("c")
    for at, g_hbm in enumerate([g2_hbm, g1_hbm]):
        @pl.when(core == at)
        def _():
            for copy in sent_out(other_ref, rest_ref, g_hbm, sems.at[at]):
                copy.wait()


def finish_other(other, g1, g2):
    return pl.pallas_call(
        other_kernel,
        in_specs=[VMEM, HBM, HBM],
        out_specs=[HBM, HBM],
        out_shape=[pltpu.HBM((WIDTH, WIDTH), F32)] * 2,
        input_output_aliases={1: 0, 2: 1},
        scratch_shapes=[pltpu.VMEM((WIDTH, WIDTH), F32), pltpu.SemaphoreType.DMA((2, 4))],
        compiler_params=pltpu.CompilerParams(vmem_limit_bytes=16 * MIB),
        name="finish_other",
    )(other, *in_hbm(g1, g2))


def exchange(rows, axes):
    parts = rows.reshape(-1, CAP, rows.shape[1])
    out = lax.all_to_all(parts, axes, split_axis=0, concat_axis=0, tiled=True)
    return out.reshape(rows.shape)


def swap(rows):
    return lax.ppermute(rows, "c", [(0, 1), (1, 0)])


def flip(rows, by):
    return lax.ppermute(rows, "x", [(i, i ^ by) for i in range(4)])


def body(embeddings, w_first, w_second, w_score, src_row, dst_owner, dst_row, edge_count, neg_ids):
    ec = edge_count.reshape(1, DEVICES)
    ws = w_score.reshape(1, WIDTH)
    src_row = src_row.reshape(1, EDGES)
    push, semb, pos = prepare(
        embeddings, src_row, dst_owner.reshape(1, EDGES), dst_row.reshape(1, EDGES), ec, neg_ids
    )
    recv = exchange(push, AXES)
    negs = pick(recv)
    negs = negs + swap(negs)
    near_x = flip(negs, 1)
    ret, gdst, rows, g1, g2, gs, loss = positive(recv, embeddings, w_first, w_second, ws, ec)
    ret, near_x = lax.optimization_barrier((ret, near_x))
    negs = negs + near_x
    negs = negs + flip(negs, 2)
    back = exchange(ret, AXES)
    keep, send, gsrc, extra = negative(semb, negs, w_first, w_second, ws, ec, g1, g2, gs, loss)
    send, back = lax.optimization_barrier((send, back))
    payload = join(keep, swap(send), extra)
    parts = exchange(payload, CHIPS)
    grads, near = scatter(gsrc, back, pos, src_row, gdst, rows, neg_ids)
    parts, grads = lax.optimization_barrier((parts, grads))
    sums = exchange(total_up(parts), CHIPS)
    other = swap(sums)
    g1, g2, gs, loss, grads = finish_own(sums, neg_ids, near, grads)
    g1, g2 = finish_other(other, g1, g2)
    return grads, g1, g2, gs.reshape(WIDTH), loss[0, 0]


def solution(mesh):
    mesh = Mesh(mesh.devices.reshape(4, 4, 2, 4), AXES)
    in_specs = (
        P(AXES, None), P(), P(), P(), P(AXES), P(AXES, None), P(AXES), P(), P(),
    )
    out_specs = (P(AXES, None), P(), P(), P(), P())
    return jax.shard_map(body, mesh=mesh, in_specs=in_specs, out_specs=out_specs, check_vma=False)
```
